32 devices in a mesh: groups: 2 (over y), blk: 16 (over z, x, core).
Axes of the slice: x: 2, y: 2, z: 4, core: 2. Of those that a mesh axis runs over, the one named last changes fastest.
Arguments:
- cell_features: bfloat16 [16384, 768], P(('groups', 'blk')), parts along dimension 0, may hold values from -6 to 6
- cell_geometry_rows: float32 [16384], P(('groups', 'blk')), parts along dimension 0, may hold values from -20 to 20
- anchor_token_features: bfloat16 [256, 768], P(('groups', 'blk')), parts along dimension 0, may hold values from -6 to 6
- anchor_geometry_rows: bfloat16 [256], P(('groups', 'blk')), parts along dimension 0, may hold values from -15 to 15
- live_anchor_count: int32 [32], P(('groups', 'blk')), parts along dimension 0, may hold values from 1 to 8, as said below
- inner_face_first: int32 [49152], P(('groups', 'blk')), parts along dimension 0, may hold values from 0 to 511
- inner_face_second: int32 [49152], P(('groups', 'blk')), parts along dimension 0, may hold values from 0 to 511
- inner_face_weight: float32 [49152], P(('groups', 'blk')), parts along dimension 0, may hold values from 0.05 to 0.4
- upper_face_cell: int32 [8192], P(('groups', 'blk')), parts along dimension 0, may hold values from 0 to 511
- lower_face_cell: int32 [8192], P(('groups', 'blk')), parts along dimension 0, may hold values from 0 to 511
- upper_face_weight: bfloat16 [8192], P(('groups', 'blk')), parts along dimension 0, may hold values from 0.049804688 to 0.3984375
- upper_slot_count: int32 [32], P(('groups', 'blk')), parts along dimension 0, may hold values from 0 to 256, as said below
- query_matrix: bfloat16 [768, 768], replicated, may hold values from -0.21875 to 0.21875
- anchor_keyvalue_matrix: bfloat16 [768, 1536], replicated, may hold values from -0.21875 to 0.21875
- output_matrix: bfloat16 [768, 768], replicated, may hold values from -0.21875 to 0.21875
- cotangent: bfloat16 [16384, 768], P(('groups', 'blk')), parts along dimension 0, may hold values from -6 to 6
Outputs:
- layer_output: bfloat16 [16384, 768], P(('groups', 'blk')), parts along dimension 0
- cell_grads: bfloat16 [16384, 768], P(('groups', 'blk')), parts along dimension 0
- weight_grads: float32 [6144, 768], P(('groups', 'blk')), parts along dimension 0
The draws below stay inside these ranges and needn't reach their ends.
There are 2 independent parts, one for each index of `groups`. The reference program is written for one: setup_inputs(seed, part) draws one part's arguments, and reference() takes and returns one part's arrays. A program takes and returns all parts, laid end to end along the dimension named above; an argument that names none is the same for every part. Nothing has to cross between parts.
Inputs may be any that keep to these rules, and one draw needn't show every extreme that they name: The live anchors of index p of blk are its first live_anchor_count[p] slots; some index has 8. Faces toward the next index of blk use the first upper_slot_count[p] slots; the last index has none; some other index has 256.
All inputs are finite; a program needn't handle non-finite values.
Results may differ from the reference program's by a relative error of at most 0.023.
Values may be sent and summed in bfloat16 or wider, within the bound.
A program may use at most 128 MiB of HBM per device.

```python
import math
import jax
import jax.numpy as jnp
from jax import lax

MODEL_WIDTH = 768
HEADS = 12
CELLS_PER_BLOCK = 512
A_DEV = 8
F_B = 256
CELLS = 8192
ANCHORS = 128
FACES_IN = 24576
IFACES = 4096
N_BLK = 16


def draw_cell_geometry_rows(key, part):
    return jnp.clip(1.5 * jax.random.normal(jax.random.fold_in(key, 4), (CELLS,), jnp.float32), -6.0, 6.0)


def draw_anchor_geometry_rows(key, part):
    return jnp.clip(jax.random.normal(jax.random.fold_in(key, 2), (ANCHORS,), jnp.float32), -4.0, 4.0).astype(jnp.bfloat16)


def draw_live_anchor_count(key, part):
    counts = jax.random.randint(jax.random.fold_in(key, 1), (N_BLK,), 1, A_DEV + 1)
    chosen = jax.random.randint(jax.random.fold_in(key, 2), (), 0, N_BLK)
    positions = jnp.arange(N_BLK, dtype=jnp.int32)
    return jnp.where(positions == chosen, A_DEV, counts).astype(jnp.int32)


def draw_upper_slot_count(key, part):
    counts = jax.random.randint(jax.random.fold_in(key, 1), (N_BLK,), F_B // 2, F_B + 1)
    chosen = jax.random.randint(jax.random.fold_in(key, 2), (), 0, N_BLK - 1)
    positions = jnp.arange(N_BLK, dtype=jnp.int32)
    counts = jnp.where(positions == chosen, F_B, counts)
    return jnp.where(positions == N_BLK - 1, 0, counts).astype(jnp.int32)


def place_ends(array, stream_key, least, top_value):
    dims = array.shape
    place = [jax.random.randint(jax.random.fold_in(stream_key, axis), (), 0, dims[axis]) for axis in range(len(dims))]
    array = array.at[tuple(place)].set(least)
    longest = dims.index(max(dims))
    place[longest] = (place[longest] + 1) % dims[longest]
    return array.at[tuple(place)].set(top_value)


def block_levels(key, extent, cuts, least, high):
    def one(dim, parts):
        draws = jax.random.uniform(jax.random.fold_in(jax.random.fold_in(key, 6), dim), (parts,), jnp.float32, least / len(cuts), high / len(cuts))
        return jnp.repeat(jnp.exp(draws), extent[dim] // parts).reshape((-1,) + (1,) * (len(extent) - dim - 1))

    factor_of = one(*cuts[0])
    for cut in cuts[1:]:
        factor_of = factor_of * one(*cut)
    return factor_of


def centred(own_key, shape, spread, most, shards=(), kind=jnp.bfloat16):
    array = spread * jax.random.normal(own_key, shape, jnp.float32)
    if shards:
        array = array * block_levels(own_key, shape, shards, -0.22, 0.18)
    return jnp.clip(array, -most, most).astype(kind)


def setup_inputs(seed: int = 0, part: int = 0) -> dict:
    key_list = jax.random.split(jax.random.key(seed), 17)
    own_keys = jax.random.split(jax.random.fold_in(key_list[16], part), 17)
    cell_features = centred(own_keys[0], (CELLS, MODEL_WIDTH), 1.0, 6.0, ((0, 16),))
    cell_geometry_rows = draw_cell_geometry_rows(jax.random.fold_in(jax.random.fold_in(key_list[16], part), 71), part)
    anchor_token_features = centred(own_keys[2], (ANCHORS, MODEL_WIDTH), 1.0, 6.0, ((0, 16),))
    anchor_geometry_rows = draw_anchor_geometry_rows(jax.random.fold_in(jax.random.fold_in(key_list[16], part), 71), part)
    live_anchor_count = draw_live_anchor_count(jax.random.fold_in(jax.random.fold_in(key_list[16], part), 71), part)
    inner_face_first = place_ends(jax.random.randint(own_keys[5], (FACES_IN,), 0, CELLS_PER_BLOCK), jax.random.fold_in(own_keys[5], 1), 0, CELLS_PER_BLOCK - 1).astype(jnp.int32)
    inner_face_second = place_ends(jax.random.randint(own_keys[6], (FACES_IN,), 0, CELLS_PER_BLOCK), jax.random.fold_in(own_keys[6], 1), 0, CELLS_PER_BLOCK - 1).astype(jnp.int32)
    inner_face_weight = jnp.clip(jnp.exp(math.log(0.4) - 2.0794415 * jax.random.uniform(own_keys[7], (FACES_IN,), jnp.float32) ** block_levels(own_keys[7], (FACES_IN,), ((0, 16),), -0.2, 0.2)), 0.05, 0.4)
    upper_face_cell = place_ends(jax.random.randint(own_keys[8], (IFACES,), 0, CELLS_PER_BLOCK), jax.random.fold_in(own_keys[8], 1), 0, CELLS_PER_BLOCK - 1).astype(jnp.int32)
    lower_face_cell = place_ends(jax.random.randint(own_keys[9], (IFACES,), 0, CELLS_PER_BLOCK), jax.random.fold_in(own_keys[9], 1), 0, CELLS_PER_BLOCK - 1).astype(jnp.int32)
    upper_face_weight = jnp.clip(jnp.exp(math.log(0.3984375) - 2.0794415 * jax.random.uniform(own_keys[10], (IFACES,), jnp.float32) ** block_levels(own_keys[10], (IFACES,), ((0, 16),), -0.2, 0.2)), 0.049804688, 0.3984375).astype(jnp.bfloat16)
    upper_slot_count = draw_upper_slot_count(jax.random.fold_in(jax.random.fold_in(key_list[16], part), 71), part)
    query_matrix = centred(key_list[12], (MODEL_WIDTH, MODEL_WIDTH), MODEL_WIDTH ** -0.5, 0.21875)
    anchor_keyvalue_matrix = centred(key_list[13], (MODEL_WIDTH, 2 * MODEL_WIDTH), MODEL_WIDTH ** -0.5, 0.21875)
    output_matrix = centred(key_list[14], (MODEL_WIDTH, MODEL_WIDTH), MODEL_WIDTH ** -0.5, 0.21875)
    cotangent = centred(own_keys[15], (CELLS, MODEL_WIDTH), 1.0, 6.0, ((0, 16),))
    return dict(cell_features=cell_features, cell_geometry_rows=cell_geometry_rows, anchor_token_features=anchor_token_features, anchor_geometry_rows=anchor_geometry_rows, live_anchor_count=live_anchor_count, inner_face_first=inner_face_first, inner_face_second=inner_face_second, inner_face_weight=inner_face_weight, upper_face_cell=upper_face_cell, lower_face_cell=lower_face_cell, upper_face_weight=upper_face_weight, upper_slot_count=upper_slot_count, query_matrix=query_matrix, anchor_keyvalue_matrix=anchor_keyvalue_matrix, output_matrix=output_matrix, cotangent=cotangent)


EPS = 1e-06

def contract(left, right, left_dim, right_dim, precision=None):
    return lax.dot_general(left, right, (((left_dim,), (right_dim,)), ((), ())), precision=precision, preferred_element_type=jnp.float32)

def face_operator(field_rows, face_lists):
    inner_face_first, inner_face_second, inner_face_weight, upper_face_cell, lower_face_cell, upper_face_weight, upper_slot_count = face_lists
    values = field_rows.astype(jnp.float32)
    offsets = (jnp.arange(N_BLK, dtype=jnp.int32) * CELLS_PER_BLOCK)[:, None]
    first_cell = (inner_face_first.reshape(N_BLK, -1) + offsets).reshape(-1)
    second_cell = (inner_face_second.reshape(N_BLK, -1) + offsets).reshape(-1)
    face_flux = inner_face_weight[:, None] * (values[second_cell] - values[first_cell])
    result = jnp.zeros_like(values).at[first_cell].add(face_flux).at[second_cell].add(-face_flux)
    upper_rows = (upper_face_cell.reshape(N_BLK, F_B) + offsets)[:-1].reshape(-1)
    lower_rows = (lower_face_cell.reshape(N_BLK, F_B) + offsets)[1:].reshape(-1)
    slot_index = jnp.arange(F_B, dtype=jnp.int32)[None, :]
    live_weight = jnp.where(slot_index < upper_slot_count[:-1, None], upper_face_weight.reshape(N_BLK, F_B).astype(jnp.float32)[:-1], 0.0).reshape(-1)
    cross_flux = live_weight[:, None] * (values[lower_rows] - values[upper_rows])
    return result.at[upper_rows].add(cross_flux).at[lower_rows].add(-cross_flux)

def reference(cell_features, cell_geometry_rows, anchor_token_features, anchor_geometry_rows, live_anchor_count, inner_face_first, inner_face_second, inner_face_weight, upper_face_cell, lower_face_cell, upper_face_weight, upper_slot_count, query_matrix, anchor_keyvalue_matrix, output_matrix, cotangent):
    head_dim = MODEL_WIDTH // HEADS
    attention_score_scale = 1.0 / math.sqrt(head_dim)
    face_lists = (inner_face_first, inner_face_second, inner_face_weight, upper_face_cell, lower_face_cell, upper_face_weight, upper_slot_count)
    mixed_rows = (cell_features.astype(jnp.float32) + face_operator(cell_features, face_lists)).astype(jnp.bfloat16)
    mixed_f = lax.optimization_barrier(mixed_rows).astype(jnp.float32)
    inverse_rms = lax.rsqrt(lax.optimization_barrier(jnp.mean(mixed_f * mixed_f, axis=1, keepdims=True)) + EPS)
    normal_hat = mixed_f * inverse_rms
    normed = normal_hat.astype(jnp.bfloat16)
    query_rows = jnp.dot(normed, query_matrix, preferred_element_type=jnp.float32).astype(jnp.bfloat16)
    keyvals = jnp.dot(anchor_token_features, anchor_keyvalue_matrix, preferred_element_type=jnp.float32).astype(jnp.bfloat16)
    key_heads = keyvals[:, :MODEL_WIDTH].reshape(ANCHORS, HEADS, head_dim).astype(jnp.float32)
    value_heads = keyvals[:, MODEL_WIDTH:].reshape(ANCHORS, HEADS, head_dim).astype(jnp.float32)
    anchor_index = jnp.arange(ANCHORS, dtype=jnp.int32)
    valid_key = anchor_index % A_DEV < jnp.repeat(live_anchor_count, A_DEV)
    anchor_geometry_code = anchor_geometry_rows.astype(jnp.float32)
    attended_gradient = contract(cotangent, output_matrix, 1, 1).astype(jnp.bfloat16)

    def block_step(grad_kv, block):
        query_blk, code_blk, grad_blk = block
        query_heads = query_blk.reshape(-1, HEADS, head_dim).astype(jnp.float32)
        attention_scores = jnp.einsum('chd,nhd->chn', query_heads, key_heads) * attention_score_scale + code_blk[:, None, None] * anchor_geometry_code[None, None, :]
        attention_scores = jnp.where(valid_key[None, None, :], attention_scores, -jnp.inf)
        row_peak = lax.optimization_barrier(jnp.max(attention_scores, axis=2, keepdims=True))
        exp_scores = jnp.exp(attention_scores - row_peak)
        prob_weights = exp_scores / lax.optimization_barrier(jnp.sum(exp_scores, axis=2, keepdims=True))
        prob_low = lax.optimization_barrier(prob_weights.astype(jnp.bfloat16)).astype(jnp.float32)
        attended = jnp.einsum('chn,nhd->chd', prob_low, value_heads).astype(jnp.bfloat16)
        grad_heads = grad_blk.reshape(-1, HEADS, head_dim).astype(jnp.float32)
        row_dot = lax.optimization_barrier(jnp.sum(grad_heads * attended.astype(jnp.float32), axis=2))
        grad_prob = jnp.einsum('chd,nhd->chn', grad_heads, value_heads)
        grad_scores = prob_weights * (grad_prob - row_dot[:, :, None])
        grad_low = lax.optimization_barrier(grad_scores.astype(jnp.bfloat16)).astype(jnp.float32)
        grad_query = (jnp.einsum('chn,nhd->chd', grad_low, key_heads) * attention_score_scale).astype(jnp.bfloat16)
        grad_key = jnp.einsum('chn,chd->nhd', grad_low, query_heads) * attention_score_scale
        grad_value = jnp.einsum('chn,chd->nhd', prob_low, grad_heads)
        grad_kv = grad_kv + jnp.concatenate([grad_key.reshape(ANCHORS, MODEL_WIDTH), grad_value.reshape(ANCHORS, MODEL_WIDTH)], axis=1)
        return (grad_kv, (attended.reshape(-1, MODEL_WIDTH), grad_query.reshape(-1, MODEL_WIDTH)))
    block_list = (query_rows.reshape(N_BLK, CELLS_PER_BLOCK, MODEL_WIDTH), cell_geometry_rows.reshape(N_BLK, CELLS_PER_BLOCK), attended_gradient.reshape(N_BLK, CELLS_PER_BLOCK, MODEL_WIDTH))
    grad_kv, outputs_all = lax.scan(block_step, jnp.zeros((ANCHORS, 2 * MODEL_WIDTH), jnp.float32), block_list)
    attended_all = outputs_all[0].reshape(-1, MODEL_WIDTH)
    grad_query_all = outputs_all[1].reshape(-1, MODEL_WIDTH)
    layer_output = (mixed_f + jnp.dot(attended_all, output_matrix, preferred_element_type=jnp.float32)).astype(jnp.bfloat16)
    grad_normed = contract(grad_query_all, query_matrix, 1, 1)
    grad_mixed = (cotangent.astype(jnp.float32) + inverse_rms * (grad_normed - normal_hat * lax.optimization_barrier(jnp.mean(grad_normed * normal_hat, axis=1, keepdims=True)))).astype(jnp.bfloat16)
    grad_mixed_f = lax.optimization_barrier(grad_mixed).astype(jnp.float32)
    cell_grads = (grad_mixed_f + face_operator(grad_mixed, face_lists)).astype(jnp.bfloat16)
    query_part = contract(grad_query_all, normed, 0, 0)
    pair_part = contract(grad_kv, anchor_token_features.astype(jnp.float32), 0, 0, lax.Precision.HIGHEST)
    output_part = contract(cotangent, attended_all, 0, 0)
    weight_grads = jnp.concatenate([query_part, pair_part, output_part], axis=0)
    return (layer_output, cell_grads, weight_grads)
```

```python
import functools
import math

import jax
import jax.numpy as jnp
from jax import lax
from jax.experimental import pallas as pl
from jax.experimental.pallas import tpu as pltpu
from jax.sharding import PartitionSpec as P

MODEL_WIDTH = 768
HEADS = 12
EPS = 1e-06
MIB = 1 << 20


def contract(left, right, left_dim, right_dim, precision=None):
    return lax.dot_general(
        left,
        right,
        (((left_dim,), (right_dim,)), ((), ())),
        precision=precision,
        preferred_element_type=jnp.float32,
    )


def exchanged(shard, bit):
    count = lax.axis_size("blk")
    return lax.ppermute(shard, "blk", [(i, i ^ bit) for i in range(count)])


def passed_along(shard, by):
    count = lax.axis_size("blk")
    return lax.ppermute(
        shard, "blk", [(i, i + by) for i in range(count) if 0 <= i + by < count]
    )


def faces_kernel(first_ref, second_ref, high_ref, low_ref, inner_high_ref, inner_low_ref):
    shape = (inner_high_ref.shape[0], first_ref.shape[1])
    ids = lax.broadcasted_iota(jnp.int32, shape, 0)
    difference = jnp.where(ids == second_ref[...], 1.0, 0.0) - jnp.where(
        ids == first_ref[...], 1.0, 0.0
    )
    low = difference.astype(jnp.bfloat16)
    total = contract((difference * high_ref[...]).astype(jnp.bfloat16), low, 1, 1)
    total = total + contract((difference * low_ref[...]).astype(jnp.bfloat16), low, 1, 1)
    high_part = (-total).astype(jnp.bfloat16)
    inner_high_ref[...] = high_part
    inner_low_ref[...] = (-total - high_part.astype(jnp.float32)).astype(jnp.bfloat16)


def inner_faces(first, second, weight, cell_count):
    high = lax.reduce_precision(weight, 8, 7)
    matrix = jax.ShapeDtypeStruct((cell_count, cell_count), jnp.bfloat16)
    slots = first.shape[0]
    return pl.pallas_call(
        faces_kernel,
        out_shape=(matrix, matrix),
        compiler_params=pltpu.CompilerParams(vmem_limit_bytes=32 * MIB),
        cost_estimate=pl.CostEstimate(
            flops=4 * slots * cell_count * cell_count,
            bytes_accessed=4 * cell_count * cell_count,
            transcendentals=0,
        ),
    )(first[None, :], second[None, :], high[None, :], (weight - high)[None, :])


def face_operator(rows, faces):
    inner_high, inner_low, cross_map, upper_live, lower_live = faces
    slots = upper_live.shape[0]
    own = contract(cross_map, rows, 0, 0)
    own_low = own.astype(jnp.bfloat16)
    peer_lower = passed_along(own_low[slots:], -1)
    peer_upper = passed_along(own_low[:slots], 1)
    inner = contract(inner_high, rows, 1, 0) + contract(inner_low, rows, 1, 0)
    upper_flux = upper_live[:, None] * (peer_lower.astype(jnp.float32) - own[:slots])
    lower_flux = lower_live[:, None] * (peer_upper.astype(jnp.float32) - own[slots:])
    flux = jnp.concatenate([upper_flux, lower_flux], axis=0).astype(jnp.bfloat16)
    return inner + contract(cross_map, flux, 1, 0)


def attention_kernel(
    scale,
    query_ref,
    grad_ref,
    key_ref,
    value_ref,
    cell_code_ref,
    anchor_code_ref,
    dead_ref,
    attended_ref,
    grad_query_ref,
    grad_key_ref,
    grad_value_ref,
):
    anchors = key_ref.shape[0]
    half = key_ref.shape[1] // 2
    left = lax.broadcasted_iota(jnp.int32, key_ref.shape, 1) < half

    def both(ref):
        rows = ref[...]
        none = jnp.zeros_like(rows)
        return jnp.concatenate([jnp.where(left, rows, none), jnp.where(left, none, rows)], axis=0)

    keys, values = both(key_ref), both(value_ref)
    queries, grads = query_ref[...], grad_ref[...]
    scores = contract(queries, keys, 1, 1)
    grad_prob = contract(grads, values, 1, 1)
    bias = cell_code_ref[...] * anchor_code_ref[...] + dead_ref[...]
    lows, grad_lows = [], []
    for head in range(2):
        part = slice(head * anchors, (head + 1) * anchors)
        score = scores[:, part] * scale + bias
        exp_scores = jnp.exp(score - jnp.max(score, axis=1, keepdims=True))
        weights = exp_scores * (1.0 / jnp.sum(exp_scores, axis=1, keepdims=True))
        low = weights.astype(jnp.bfloat16)
        gradient = grad_prob[:, part]
        dots = jnp.sum(low.astype(jnp.float32) * gradient, axis=1, keepdims=True)
        lows.append(low)
        grad_lows.append((weights * (gradient - dots)).astype(jnp.bfloat16))
    low = jnp.concatenate(lows, axis=1)
    grad_low = jnp.concatenate(grad_lows, axis=1)
    attended_ref[...] = contract(low, values, 1, 0).astype(jnp.bfloat16)
    grad_query_ref[...] = (contract(grad_low, keys, 1, 0) * scale).astype(jnp.bfloat16)
    upper = lax.broadcasted_iota(jnp.int32, grad_key_ref.shape, 0) < half
    grad_key = contract(queries, grad_low, 0, 0) * scale
    grad_key_ref[...] = jnp.where(upper, grad_key[:, :anchors], grad_key[:, anchors:])
    grad_value = contract(grads, low, 0, 0)
    grad_value_ref[...] = jnp.where(upper, grad_value[:, :anchors], grad_value[:, anchors:])


def attention(queries, grads, keyvals, cell_code, anchor_code, dead):
    cells = queries.shape[0]
    anchors = keyvals.shape[0]
    pairs = HEADS // 2
    wide = MODEL_WIDTH // pairs
    rows = pl.BlockSpec((cells, wide), lambda i: (0, i))
    keys = pl.BlockSpec((anchors, wide), lambda i: (0, i))
    values = pl.BlockSpec((anchors, wide), lambda i: (0, i + pairs))
    turned = pl.BlockSpec((wide, anchors), lambda i: (i, 0))
    fixed = lambda shape: pl.BlockSpec(shape, lambda i: (0, 0))
    limit = min(56 * MIB, 16 * MIB + 64 * cells * anchors)
    return pl.pallas_call(
        functools.partial(attention_kernel, 1.0 / math.sqrt(MODEL_WIDTH // HEADS)),
        grid=(pairs,),
        in_specs=[rows, rows, keys, values, fixed((cells, 1)), fixed((1, anchors)), fixed((1, anchors))],
        out_specs=[rows, rows, turned, turned],
        out_shape=(
            jax.ShapeDtypeStruct((cells, MODEL_WIDTH), jnp.bfloat16),
            jax.ShapeDtypeStruct((cells, MODEL_WIDTH), jnp.bfloat16),
            jax.ShapeDtypeStruct((MODEL_WIDTH, anchors), jnp.float32),
            jax.ShapeDtypeStruct((MODEL_WIDTH, anchors), jnp.float32),
        ),
        compiler_params=pltpu.CompilerParams(vmem_limit_bytes=limit),
        cost_estimate=pl.CostEstimate(
            flops=24 * cells * anchors * MODEL_WIDTH,
            bytes_accessed=8 * cells * MODEL_WIDTH,
            transcendentals=cells * anchors * HEADS,
        ),
    )(queries, grads, keyvals, keyvals, cell_code[:, None], anchor_code[None, :], dead[None, :])


def gathered(rows):
    me = lax.axis_index("blk")
    bit = 1
    while bit < lax.axis_size("blk"):
        peer = exchanged(rows, bit)
        upper = (me & bit) > 0
        rows = jnp.concatenate(
            [jnp.where(upper, peer, rows), jnp.where(upper, rows, peer)], axis=0
        )
        bit *= 2
    return rows


def halved(blocks, quarter):
    me = lax.axis_index("blk")
    bit = 1
    while bit < quarter:
        shape = blocks.shape
        paired = blocks.reshape(shape[0], shape[1] // 2, 2, shape[2], shape[3])
        upper = (me & bit) > 0
        sent = jnp.where(upper, paired[:, :, 0], paired[:, :, 1]).astype(jnp.bfloat16)
        kept = jnp.where(upper, paired[:, :, 1], paired[:, :, 0])
        blocks = kept + exchanged(sent, bit).astype(jnp.float32)
        bit *= 2
    return blocks[:, 0]


def summed_weight_grads(query_part, pair_left, output_part, tokens):
    count = lax.axis_size("blk")
    me = lax.axis_index("blk")
    quarter = count // 4
    rows = 4 * MODEL_WIDTH // count
    output_block = halved(output_part.reshape(1, quarter, rows, MODEL_WIDTH), quarter)[0]
    pair_blocks = halved(pair_left.reshape(2, quarter, rows, -1), quarter)
    query_block = halved(query_part.reshape(1, quarter, rows, MODEL_WIDTH), quarter)[0]
    place = me // quarter
    odd = place % 2 > 0
    pair_sent = jnp.where(odd, pair_blocks[1], pair_blocks[0]).astype(jnp.bfloat16)
    pair_kept = jnp.where(odd, pair_blocks[0], pair_blocks[1])
    pair = pair_kept + exchanged(pair_sent, quarter).astype(jnp.float32)
    sent = jnp.where(odd, query_block, output_block).astype(jnp.bfloat16)
    kept = jnp.where(odd, output_block, query_block)
    block = kept + exchanged(sent, quarter).astype(jnp.float32)
    inward = [(i, i + 2 * quarter) for i in range(quarter)]
    inward += [(i, i - 2 * quarter) for i in range(3 * quarter, count)]
    outward = [(to, start) for start, to in inward]
    pair = pair + lax.ppermute(pair.astype(jnp.bfloat16), "blk", inward).astype(jnp.float32)
    block = block + lax.ppermute(block.astype(jnp.bfloat16), "blk", outward).astype(jnp.float32)
    product = contract(pair, tokens.astype(jnp.float32), 1, 0, lax.Precision.HIGHEST)
    return jnp.where((place == 0) | (place == 3), block, product)


def shards(
    cell_features,
    cell_geometry_rows,
    anchor_token_features,
    anchor_geometry_rows,
    live_anchor_count,
    inner_face_first,
    inner_face_second,
    inner_face_weight,
    upper_face_cell,
    lower_face_cell,
    upper_face_weight,
    upper_slot_count,
    query_matrix,
    anchor_keyvalue_matrix,
    output_matrix,
    cotangent,
):
    cell_count = cell_features.shape[0]
    own_anchors = anchor_token_features.shape[0]
    slot_index = jnp.arange(upper_face_cell.shape[0], dtype=jnp.int32)
    live_weight = jnp.where(slot_index < upper_slot_count[0], upper_face_weight, 0).astype(
        jnp.bfloat16
    )
    lower_live = passed_along(live_weight, 1).astype(jnp.float32)
    live = jnp.arange(own_anchors, dtype=jnp.int32) < live_anchor_count[0]
    side = jnp.stack([anchor_geometry_rows, live.astype(jnp.bfloat16)], axis=1)
    packed = gathered(
        jnp.concatenate([anchor_token_features, jnp.pad(side, ((0, 0), (0, 126)))], axis=1)
    )
    tokens = packed[:, :MODEL_WIDTH]
    anchor_code = packed[:, MODEL_WIDTH].astype(jnp.float32)
    dead = jnp.where(packed[:, MODEL_WIDTH + 1] > 0, 0.0, -jnp.inf).astype(jnp.float32)

    cell_ids = jnp.arange(cell_count, dtype=jnp.int32)
    cross_cells = jnp.concatenate([upper_face_cell, lower_face_cell])
    cross_map = (cell_ids[:, None] == cross_cells[None, :]).astype(jnp.bfloat16)
    faces = inner_faces(inner_face_first, inner_face_second, inner_face_weight, cell_count) + (
        cross_map,
        live_weight.astype(jnp.float32),
        lower_live,
    )
    mixed_rows = (
        cell_features.astype(jnp.float32) + face_operator(cell_features, faces)
    ).astype(jnp.bfloat16)
    mixed_f = lax.optimization_barrier(mixed_rows).astype(jnp.float32)
    inverse_rms = lax.rsqrt(jnp.mean(mixed_f * mixed_f, axis=1, keepdims=True) + EPS)
    normal_hat = mixed_f * inverse_rms
    normed = normal_hat.astype(jnp.bfloat16)
    queries = contract(normed, query_matrix, 1, 0).astype(jnp.bfloat16)
    keyvals = contract(tokens, anchor_keyvalue_matrix, 1, 0).astype(jnp.bfloat16)
    attended_gradient = contract(cotangent, output_matrix, 1, 1).astype(jnp.bfloat16)
    attended, grad_queries, grad_keys, grad_values = attention(
        queries, attended_gradient, keyvals, cell_geometry_rows, anchor_code, dead
    )
    grad_normed = contract(grad_queries, query_matrix, 1, 1)
    grad_mixed = (
        cotangent.astype(jnp.float32)
        + inverse_rms
        * (grad_normed - normal_hat * jnp.mean(grad_normed * normal_hat, axis=1, keepdims=True))
    ).astype(jnp.bfloat16)
    grad_mixed = lax.optimization_barrier(grad_mixed)
    weight_grads = summed_weight_grads(
        contract(grad_queries, normed, 0, 0),
        jnp.stack([grad_keys, grad_values]),
        contract(cotangent, attended, 0, 0),
        tokens,
    )
    cell_grads = (grad_mixed.astype(jnp.float32) + face_operator(grad_mixed, faces)).astype(
        jnp.bfloat16
    )
    layer_output = (mixed_f + contract(attended, output_matrix, 1, 0)).astype(jnp.bfloat16)
    return (layer_output, cell_grads, weight_grads)


def solution(mesh):
    cells = P(("groups", "blk"))
    in_specs = (cells,) * 12 + (P(), P(), P(), cells)
    return jax.shard_map(
        shards, mesh=mesh, in_specs=in_specs, out_specs=(cells, cells, cells), check_vma=False
    )
```

```python
import functools
import math

import jax
import jax.numpy as jnp
from jax import lax
from jax.experimental import pallas as pl
from jax.experimental.pallas import tpu as pltpu
from jax.sharding import PartitionSpec as P

MODEL_WIDTH = 768
HEADS = 12
EPS = 1e-06
MIB = 1 << 20
MESH = pl.DeviceIdType.MESH


def contract(left, right, left_dim, right_dim, precision=None):
    return lax.dot_general(
        left,
        right,
        (((left_dim,), (right_dim,)), ((), ())),
        precision=precision,
        preferred_element_type=jnp.float32,
    )


def exchanged(shard, bit):
    count = lax.axis_size("blk")
    return lax.ppermute(shard, "blk", [(i, i ^ bit) for i in range(count)])


def passed_along(shard, by):
    count = lax.axis_size("blk")
    return lax.ppermute(
        shard, "blk", [(i, i + by) for i in range(count) if 0 <= i + by < count]
    )


def front_kernel(
    count,
    cells_ref,
    first_ref,
    second_ref,
    high_ref,
    low_ref,
    cross_ref,
    live_ref,
    pack_ref,
    mixed_ref,
    normed_ref,
    inverse_ref,
    inner_high_ref,
    inner_low_ref,
    cross_map_ref,
    weighted_map_ref,
    gathered_ref,
    own,
    peer,
    lower_live,
    landed,
    pack_send,
    pack_recv,
    face_send,
    face_recv,
):
    me = lax.axis_index("blk")
    slots = live_ref.shape[1]
    cell_count = cells_ref.shape[0]
    barrier = pltpu.get_barrier_semaphore()

    def greet(step, carry):
        pl.semaphore_signal(
            barrier, inc=1, device_id={"blk": lax.rem(me + step, count)}, device_id_type=MESH
        )
        return carry

    lax.fori_loop(1, count, greet, 0)
    ids = lax.broadcasted_iota(jnp.int32, (cell_count, 2 * slots), 0)
    cross_map = jnp.where(ids == cross_ref[...], 1.0, 0.0)
    cross_map_ref[...] = cross_map.astype(jnp.bfloat16)
    rows = cells_ref[...]
    chosen = contract(cross_map_ref[...], rows, 0, 0)
    own[0] = chosen[:slots].astype(jnp.bfloat16)
    own[1] = chosen[slots:].astype(jnp.bfloat16)
    pl.semaphore_wait(barrier, count - 1)

    def sent(source, target, place, by):
        return pltpu.make_async_remote_copy(
            src_ref=source,
            dst_ref=target,
            send_sem=face_send.at[place],
            recv_sem=face_recv.at[place],
            device_id={"blk": lax.rem(me + by + count, count)},
            device_id_type=MESH,
        )

    down = sent(own.at[1], peer.at[0], 0, -1)
    up = sent(own.at[0], peer.at[1], 1, 1)
    weights = sent(live_ref, lower_live, 2, 1)

    @pl.when(me > 0)
    def _():
        down.start()

    @pl.when(me < count - 1)
    def _():
        up.start()
        weights.start()

    def pack_copy(step, place):
        return pltpu.make_async_remote_copy(
            src_ref=pack_ref,
            dst_ref=landed.at[place],
            send_sem=pack_send.at[step],
            recv_sem=pack_recv.at[place],
            device_id={"blk": lax.rem(me + step, count)},
            device_id_type=MESH,
        )

    def send_pack(step, carry):
        pack_copy(step, me).start()
        return carry

    lax.fori_loop(1, count, send_pack, 0)
    landed[me] = pack_ref[...]

    @pl.when(me == 0)
    def _():
        peer[1] = jnp.zeros(peer.shape[1:], peer.dtype)
        lower_live[...] = jnp.zeros_like(lower_live)

    @pl.when(me == count - 1)
    def _():
        peer[0] = jnp.zeros(peer.shape[1:], peer.dtype)

    shape = (cell_count, first_ref.shape[1])
    ids = lax.broadcasted_iota(jnp.int32, shape, 0)
    difference = jnp.where(ids == second_ref[...], 1.0, 0.0) - jnp.where(
        ids == first_ref[...], 1.0, 0.0
    )
    low = difference.astype(jnp.bfloat16)
    total = contract((difference * high_ref[...]).astype(jnp.bfloat16), low, 1, 1)
    total = total + contract((difference * low_ref[...]).astype(jnp.bfloat16), low, 1, 1)
    high_part = (-total).astype(jnp.bfloat16)
    inner_high_ref[...] = high_part
    inner_low_ref[...] = (-total - high_part.astype(jnp.float32)).astype(jnp.bfloat16)
    inner = contract(inner_high_ref[...], rows, 1, 0) + contract(inner_low_ref[...], rows, 1, 0)

    @pl.when(me < count - 1)
    def _():
        down.wait_recv()
        up.wait_send()
        weights.wait_send()

    @pl.when(me > 0)
    def _():
        up.wait_recv()
        weights.wait_recv()
        down.wait_send()

    live = jnp.concatenate([live_ref[...][:1], lower_live[...][:1]], axis=1)
    weighted_map_ref[...] = (cross_map_ref[...].astype(jnp.float32) * live).astype(jnp.bfloat16)
    flux = jnp.concatenate(
        [
            (peer[0].astype(jnp.float32) - own[0].astype(jnp.float32)).astype(jnp.bfloat16),
            (peer[1].astype(jnp.float32) - own[1].astype(jnp.float32)).astype(jnp.bfloat16),
        ],
        axis=0,
    )
    mixed = (
        rows.astype(jnp.float32) + inner + contract(weighted_map_ref[...], flux, 1, 0)
    ).astype(jnp.bfloat16)
    mixed_ref[...] = mixed
    mixed = mixed.astype(jnp.float32)
    inverse = lax.rsqrt(jnp.mean(mixed * mixed, axis=1, keepdims=True) + EPS)
    inverse_ref[...] = inverse
    normed_ref[...] = (mixed * inverse).astype(jnp.bfloat16)

    def take_pack(step, carry):
        pack_copy(step, lax.rem(me + count - step, count)).wait_recv()
        pack_copy(step, me).wait_send()
        return carry

    lax.fori_loop(1, count, take_pack, 0)
    gathered_ref[...] = landed[...]


def front(cells, first, second, weight, cross_cells, live, pack):
    count = lax.axis_size("blk")
    cell_count = cells.shape[0]
    slots = live.shape[0]
    high = lax.reduce_precision(weight, 8, 7)
    low_type = lambda *shape: jax.ShapeDtypeStruct(shape, jnp.bfloat16)
    return pl.pallas_call(
        functools.partial(front_kernel, count),
        in_specs=[pl.BlockSpec(memory_space=pltpu.VMEM)] * 8,
        out_specs=[pl.BlockSpec(memory_space=pltpu.VMEM)] * 8,
        out_shape=(
            low_type(*cells.shape),
            low_type(*cells.shape),
            jax.ShapeDtypeStruct((cell_count, 1), jnp.float32),
            low_type(cell_count, cell_count),
            low_type(cell_count, cell_count),
            low_type(cell_count, 2 * slots),
            low_type(cell_count, 2 * slots),
            low_type(count, *pack.shape),
        ),
        scratch_shapes=[
            pltpu.VMEM((2, slots, cells.shape[1]), jnp.bfloat16),
            pltpu.VMEM((2, slots, cells.shape[1]), jnp.bfloat16),
            pltpu.VMEM((8, slots), jnp.float32),
            pltpu.VMEM((count, *pack.shape), jnp.bfloat16),
            pltpu.SemaphoreType.DMA((count,)),
            pltpu.SemaphoreType.DMA((count,)),
            pltpu.SemaphoreType.DMA((3,)),
            pltpu.SemaphoreType.DMA((3,)),
        ],
        compiler_params=pltpu.CompilerParams(
            collective_id=0, has_side_effects=True, vmem_limit_bytes=40 * MIB
        ),
        cost_estimate=pl.CostEstimate(
            flops=8 * first.shape[0] * cell_count * cell_count,
            bytes_accessed=8 * cell_count * cell_count,
            transcendentals=0,
        ),
    )(
        cells,
        first[None, :],
        second[None, :],
        high[None, :],
        (weight - high)[None, :],
        cross_cells[None, :],
        jnp.broadcast_to(live[None, :], (8, slots)),
        pack,
    )


def face_operator(rows, faces):
    inner_high, inner_low, cross_map, weighted_map = faces
    slots = cross_map.shape[1] // 2
    own = contract(cross_map, rows, 0, 0)
    own_low = own.astype(jnp.bfloat16)
    peer_lower = passed_along(own_low[slots:], -1)
    peer_upper = passed_along(own_low[:slots], 1)
    inner = contract(inner_high, rows, 1, 0) + contract(inner_low, rows, 1, 0)
    peers = jnp.concatenate([peer_lower, peer_upper], axis=0)
    flux = (peers.astype(jnp.float32) - own).astype(jnp.bfloat16)
    return inner + contract(weighted_map, flux, 1, 0)


def attention_kernel(
    scale,
    query_ref,
    grad_ref,
    key_ref,
    value_ref,
    cell_code_ref,
    anchor_code_ref,
    dead_ref,
    attended_ref,
    grad_query_ref,
    grad_key_ref,
    grad_value_ref,
):
    anchors = key_ref.shape[0]
    half = key_ref.shape[1] // 2
    left = lax.broadcasted_iota(jnp.int32, key_ref.shape, 1) < half

    def both(ref):
        rows = ref[...]
        none = jnp.zeros_like(rows)
        return jnp.concatenate([jnp.where(left, rows, none), jnp.where(left, none, rows)], axis=0)

    keys, values = both(key_ref), both(value_ref)
    queries, grads = query_ref[...], grad_ref[...]
    scores = contract(queries, keys, 1, 1)
    grad_prob = contract(grads, values, 1, 1)
    bias = cell_code_ref[...] * anchor_code_ref[...] + dead_ref[...]
    lows, grad_lows = [], []
    for head in range(2):
        part = slice(head * anchors, (head + 1) * anchors)
        score = scores[:, part] * scale + bias
        exp_scores = jnp.exp(score - jnp.max(score, axis=1, keepdims=True))
        weights = exp_scores * (1.0 / jnp.sum(exp_scores, axis=1, keepdims=True))
        low = weights.astype(jnp.bfloat16)
        gradient = grad_prob[:, part]
        dots = jnp.sum(low.astype(jnp.float32) * gradient, axis=1, keepdims=True)
        lows.append(low)
        grad_lows.append((weights * (gradient - dots)).astype(jnp.bfloat16))
    low = jnp.concatenate(lows, axis=1)
    grad_low = jnp.concatenate(grad_lows, axis=1)
    attended_ref[...] = contract(low, values, 1, 0).astype(jnp.bfloat16)
    grad_query_ref[...] = (contract(grad_low, keys, 1, 0) * scale).astype(jnp.bfloat16)
    upper = lax.broadcasted_iota(jnp.int32, grad_key_ref.shape, 0) < half
    grad_key = contract(queries, grad_low, 0, 0) * scale
    grad_key_ref[...] = jnp.where(upper, grad_key[:, :anchors], grad_key[:, anchors:])
    grad_value = contract(grads, low, 0, 0)
    grad_value_ref[...] = jnp.where(upper, grad_value[:, :anchors], grad_value[:, anchors:])


def attention(queries, grads, keyvals, cell_code, anchor_code, dead):
    cells = queries.shape[0]
    anchors = keyvals.shape[0]
    pairs = HEADS // 2
    wide = MODEL_WIDTH // pairs
    rows = pl.BlockSpec((cells, wide), lambda i: (0, i))
    keys = pl.BlockSpec((anchors, wide), lambda i: (0, i))
    values = pl.BlockSpec((anchors, wide), lambda i: (0, i + pairs))
    turned = pl.BlockSpec((wide, anchors), lambda i: (i, 0))
    fixed = lambda shape: pl.BlockSpec(shape, lambda i: (0, 0))
    limit = min(56 * MIB, 16 * MIB + 64 * cells * anchors)
    return pl.pallas_call(
        functools.partial(attention_kernel, 1.0 / math.sqrt(MODEL_WIDTH // HEADS)),
        grid=(pairs,),
        in_specs=[rows, rows, keys, values, fixed((cells, 1)), fixed((1, anchors)), fixed((1, anchors))],
        out_specs=[rows, rows, turned, turned],
        out_shape=(
            jax.ShapeDtypeStruct((cells, MODEL_WIDTH), jnp.bfloat16),
            jax.ShapeDtypeStruct((cells, MODEL_WIDTH), jnp.bfloat16),
            jax.ShapeDtypeStruct((MODEL_WIDTH, anchors), jnp.float32),
            jax.ShapeDtypeStruct((MODEL_WIDTH, anchors), jnp.float32),
        ),
        compiler_params=pltpu.CompilerParams(vmem_limit_bytes=limit),
        cost_estimate=pl.CostEstimate(
            flops=24 * cells * anchors * MODEL_WIDTH,
            bytes_accessed=8 * cells * MODEL_WIDTH,
            transcendentals=cells * anchors * HEADS,
        ),
    )(queries, grads, keyvals, keyvals, cell_code[:, None], anchor_code[None, :], dead[None, :])


def halved(blocks, quarter):
    me = lax.axis_index("blk")
    bit = 1
    while bit < quarter:
        shape = blocks.shape
        paired = blocks.reshape(shape[0], shape[1] // 2, 2, shape[2], shape[3])
        upper = (me & bit) > 0
        sent = jnp.where(upper, paired[:, :, 0], paired[:, :, 1]).astype(jnp.bfloat16)
        kept = jnp.where(upper, paired[:, :, 1], paired[:, :, 0])
        blocks = kept + exchanged(sent, bit).astype(jnp.float32)
        bit *= 2
    return blocks[:, 0]


def summed_weight_grads(query_part, pair_left, output_part, tokens):
    count = lax.axis_size("blk")
    me = lax.axis_index("blk")
    quarter = count // 4
    rows = 4 * MODEL_WIDTH // count
    output_block = halved(output_part.reshape(1, quarter, rows, MODEL_WIDTH), quarter)[0]
    pair_blocks = halved(pair_left.reshape(2, quarter, rows, -1), quarter)
    query_block = halved(query_part.reshape(1, quarter, rows, MODEL_WIDTH), quarter)[0]
    place = me // quarter
    odd = place % 2 > 0
    pair_sent = jnp.where(odd, pair_blocks[1], pair_blocks[0]).astype(jnp.bfloat16)
    pair_kept = jnp.where(odd, pair_blocks[0], pair_blocks[1])
    pair = pair_kept + exchanged(pair_sent, quarter).astype(jnp.float32)
    sent = jnp.where(odd, query_block, output_block).astype(jnp.bfloat16)
    kept = jnp.where(odd, output_block, query_block)
    block = kept + exchanged(sent, quarter).astype(jnp.float32)
    inward = [(i, i + 2 * quarter) for i in range(quarter)]
    inward += [(i, i - 2 * quarter) for i in range(3 * quarter, count)]
    outward = [(to, start) for start, to in inward]
    pair = pair + lax.ppermute(pair.astype(jnp.bfloat16), "blk", inward).astype(jnp.float32)
    block = block + lax.ppermute(block.astype(jnp.bfloat16), "blk", outward).astype(jnp.float32)
    product = contract(pair, tokens.astype(jnp.float32), 1, 0, lax.Precision.HIGHEST)
    return jnp.where((place == 0) | (place == 3), block, product)


def shards(
    cell_features,
    cell_geometry_rows,
    anchor_token_features,
    anchor_geometry_rows,
    live_anchor_count,
    inner_face_first,
    inner_face_second,
    inner_face_weight,
    upper_face_cell,
    lower_face_cell,
    upper_face_weight,
    upper_slot_count,
    query_matrix,
    anchor_keyvalue_matrix,
    output_matrix,
    cotangent,
):
    own_anchors = anchor_token_features.shape[0]
    slot_index = jnp.arange(upper_face_cell.shape[0], dtype=jnp.int32)
    live_weight = jnp.where(
        slot_index < upper_slot_count[0], upper_face_weight.astype(jnp.float32), 0.0
    )
    live = jnp.arange(own_anchors, dtype=jnp.int32) < live_anchor_count[0]
    side = jnp.concatenate([anchor_geometry_rows, live.astype(jnp.bfloat16)])
    half_width = MODEL_WIDTH // 2
    pack = jnp.concatenate(
        [
            anchor_token_features.reshape(2 * own_anchors, half_width),
            jnp.broadcast_to(side[:, None], (2 * own_anchors, 128)),
        ],
        axis=1,
    )
    mixed_rows, normed, inverse_rms, inner_high, inner_low, cross_map, weighted_map, packed = front(
        cell_features,
        inner_face_first,
        inner_face_second,
        inner_face_weight,
        jnp.concatenate([upper_face_cell, lower_face_cell]),
        live_weight,
        pack,
    )
    faces = (inner_high, inner_low, cross_map, weighted_map)
    tokens = packed[:, :, :half_width].reshape(-1, MODEL_WIDTH)
    anchor_code = packed[:, :own_anchors, half_width].reshape(-1).astype(jnp.float32)
    dead = jnp.where(packed[:, own_anchors:, half_width] > 0, 0.0, -jnp.inf)
    dead = dead.reshape(-1).astype(jnp.float32)
    mixed_f = mixed_rows.astype(jnp.float32)
    normal_hat = mixed_f * inverse_rms
    queries = contract(normed, query_matrix, 1, 0).astype(jnp.bfloat16)
    keyvals = contract(tokens, anchor_keyvalue_matrix, 1, 0).astype(jnp.bfloat16)
    attended_gradient = contract(cotangent, output_matrix, 1, 1).astype(jnp.bfloat16)
    attended, grad_queries, grad_keys, grad_values = attention(
        queries, attended_gradient, keyvals, cell_geometry_rows, anchor_code, dead
    )
    grad_normed = contract(grad_queries, query_matrix, 1, 1)
    grad_mixed = (
        cotangent.astype(jnp.float32)
        + inverse_rms
        * (grad_normed - normal_hat * jnp.mean(grad_normed * normal_hat, axis=1, keepdims=True))
    ).astype(jnp.bfloat16)
    grad_mixed = lax.optimization_barrier(grad_mixed)
    weight_grads = summed_weight_grads(
        contract(grad_queries, normed, 0, 0),
        jnp.stack([grad_keys, grad_values]),
        contract(cotangent, attended, 0, 0),
        tokens,
    )
    cell_grads = (grad_mixed.astype(jnp.float32) + face_operator(grad_mixed, faces)).astype(
        jnp.bfloat16
    )
    layer_output = (mixed_f + contract(attended, output_matrix, 1, 0)).astype(jnp.bfloat16)
    return (layer_output, cell_grads, weight_grads)


def solution(mesh):
    cells = P(("groups", "blk"))
    in_specs = (cells,) * 12 + (P(), P(), P(), cells)
    return jax.shard_map(
        shards, mesh=mesh, in_specs=in_specs, out_specs=(cells, cells, cells), check_vma=False
    )
```

```python
import functools
import math

import jax
import jax.numpy as jnp
from jax import lax
from jax.experimental import pallas as pl
from jax.experimental.pallas import tpu as pltpu
from jax.sharding import PartitionSpec as P

MODEL_WIDTH = 768
HEADS = 12
EPS = 1e-06
MIB = 1 << 20
MESH = pl.DeviceIdType.MESH


def contract(left, right, left_dim, right_dim, precision=None):
    return lax.dot_general(
        left,
        right,
        (((left_dim,), (right_dim,)), ((), ())),
        precision=precision,
        preferred_element_type=jnp.float32,
    )


def exchanged(shard, bit):
    count = lax.axis_size("blk")
    return lax.ppermute(shard, "blk", [(i, i ^ bit) for i in range(count)])


def passed_along(shard, by):
    count = lax.axis_size("blk")
    return lax.ppermute(
        shard, "blk", [(i, i + by) for i in range(count) if 0 <= i + by < count]
    )


def front_kernel(
    count,
    cells_ref,
    inner_ref,
    cross_ref,
    pack_ref,
    mixed_ref,
    normed_ref,
    inverse_ref,
    inner_high_ref,
    inner_low_ref,
    cross_map_ref,
    weighted_map_ref,
    gathered_ref,
    own,
    peer,
    lower_live,
    landed,
    pack_send,
    pack_recv,
    face_send,
    face_recv,
):
    me = lax.axis_index("blk")
    slots = cross_ref.shape[1] // 2
    live_ref = cross_ref.at[:, pl.ds(0, slots)]
    cell_count = cells_ref.shape[0]
    barrier = pltpu.get_barrier_semaphore()

    def greet(step, carry):
        pl.semaphore_signal(
            barrier, inc=1, device_id={"blk": lax.rem(me + step, count)}, device_id_type=MESH
        )
        return carry

    lax.fori_loop(1, count, greet, 0)
    ids = lax.broadcasted_iota(jnp.int32, (cell_count, 2 * slots), 0)
    cross_map = jnp.where(ids == cross_ref[...][:1].astype(jnp.int32), 1.0, 0.0)
    cross_map_ref[...] = cross_map.astype(jnp.bfloat16)
    rows = cells_ref[...]
    chosen = contract(cross_map_ref[...], rows, 0, 0)
    own[0] = chosen[:slots].astype(jnp.bfloat16)
    own[1] = chosen[slots:].astype(jnp.bfloat16)
    pl.semaphore_wait(barrier, count - 1)

    def sent(source, target, place, by):
        return pltpu.make_async_remote_copy(
            src_ref=source,
            dst_ref=target,
            send_sem=face_send.at[place],
            recv_sem=face_recv.at[place],
            device_id={"blk": lax.rem(me + by + count, count)},
            device_id_type=MESH,
        )

    down = sent(own.at[1], peer.at[0], 0, -1)
    up = sent(own.at[0], peer.at[1], 1, 1)
    weights = sent(live_ref, lower_live, 2, 1)

    @pl.when(me > 0)
    def _():
        down.start()

    @pl.when(me < count - 1)
    def _():
        up.start()
        weights.start()

    def pack_copy(step, place):
        return pltpu.make_async_remote_copy(
            src_ref=pack_ref,
            dst_ref=landed.at[place],
            send_sem=pack_send.at[step],
            recv_sem=pack_recv.at[place],
            device_id={"blk": lax.rem(me + step, count)},
            device_id_type=MESH,
        )

    def send_pack(step, carry):
        pack_copy(step, me).start()
        return carry

    lax.fori_loop(1, count, send_pack, 0)
    landed[me] = pack_ref[...]

    @pl.when(me == 0)
    def _():
        peer[1] = jnp.zeros(peer.shape[1:], peer.dtype)
        lower_live[...] = jnp.zeros_like(lower_live)

    @pl.when(me == count - 1)
    def _():
        peer[0] = jnp.zeros(peer.shape[1:], peer.dtype)

    inner_rows = inner_ref[...]
    first, second = inner_rows[:1].astype(jnp.int32), inner_rows[1:2].astype(jnp.int32)
    weight = inner_rows[2:3]
    weight_high = weight.astype(jnp.bfloat16).astype(jnp.float32)
    weight_low = weight - weight_high
    ids = lax.broadcasted_iota(jnp.int32, (cell_count, inner_ref.shape[1]), 0)
    difference = jnp.where(ids == second, 1.0, 0.0) - jnp.where(ids == first, 1.0, 0.0)
    low = difference.astype(jnp.bfloat16)
    total = contract((difference * weight_high).astype(jnp.bfloat16), low, 1, 1)
    total = total + contract((difference * weight_low).astype(jnp.bfloat16), low, 1, 1)
    high_part = (-total).astype(jnp.bfloat16)
    inner_high_ref[...] = high_part
    inner_low_ref[...] = (-total - high_part.astype(jnp.float32)).astype(jnp.bfloat16)
    inner = contract(inner_high_ref[...], rows, 1, 0) + contract(inner_low_ref[...], rows, 1, 0)

    @pl.when(me < count - 1)
    def _():
        down.wait_recv()
        up.wait_send()
        weights.wait_send()

    @pl.when(me > 0)
    def _():
        up.wait_recv()
        weights.wait_recv()
        down.wait_send()

    live = jnp.concatenate(
        [cross_ref[...][1:2, :slots], lower_live[...][1:2]], axis=1
    )
    weighted_map_ref[...] = (cross_map_ref[...].astype(jnp.float32) * live).astype(jnp.bfloat16)
    flux = jnp.concatenate(
        [
            (peer[0].astype(jnp.float32) - own[0].astype(jnp.float32)).astype(jnp.bfloat16),
            (peer[1].astype(jnp.float32) - own[1].astype(jnp.float32)).astype(jnp.bfloat16),
        ],
        axis=0,
    )
    mixed = (
        rows.astype(jnp.float32) + inner + contract(weighted_map_ref[...], flux, 1, 0)
    ).astype(jnp.bfloat16)
    mixed_ref[...] = mixed
    mixed = mixed.astype(jnp.float32)
    inverse = lax.rsqrt(jnp.mean(mixed * mixed, axis=1, keepdims=True) + EPS)
    inverse_ref[...] = inverse
    normed_ref[...] = (mixed * inverse).astype(jnp.bfloat16)

    def take_pack(step, carry):
        pack_copy(step, lax.rem(me + count - step, count)).wait_recv()
        pack_copy(step, me).wait_send()
        return carry

    lax.fori_loop(1, count, take_pack, 0)
    gathered_ref[...] = landed[...]


def front(cells, first, second, weight, cross_cells, live, pack):
    count = lax.axis_size("blk")
    cell_count = cells.shape[0]
    slots = live.shape[0]
    inner_table = jnp.concatenate(
        [
            first.astype(jnp.float32)[None, :],
            second.astype(jnp.float32)[None, :],
            weight[None, :],
            jnp.zeros((5, first.shape[0]), jnp.float32),
        ],
        axis=0,
    )
    cross_table = jnp.concatenate(
        [
            cross_cells.astype(jnp.float32)[None, :],
            jnp.pad(live, (0, slots))[None, :],
            jnp.zeros((6, 2 * slots), jnp.float32),
        ],
        axis=0,
    )
    low_type = lambda *shape: jax.ShapeDtypeStruct(shape, jnp.bfloat16)
    return pl.pallas_call(
        functools.partial(front_kernel, count),
        in_specs=[pl.BlockSpec(memory_space=pltpu.VMEM)] * 4,
        out_specs=[pl.BlockSpec(memory_space=pltpu.VMEM)] * 8,
        out_shape=(
            low_type(*cells.shape),
            low_type(*cells.shape),
            jax.ShapeDtypeStruct((cell_count, 1), jnp.float32),
            low_type(cell_count, cell_count),
            low_type(cell_count, cell_count),
            low_type(cell_count, 2 * slots),
            low_type(cell_count, 2 * slots),
            low_type(count, *pack.shape),
        ),
        scratch_shapes=[
            pltpu.VMEM((2, slots, cells.shape[1]), jnp.bfloat16),
            pltpu.VMEM((2, slots, cells.shape[1]), jnp.bfloat16),
            pltpu.VMEM((8, slots), jnp.float32),
            pltpu.VMEM((count, *pack.shape), jnp.bfloat16),
            pltpu.SemaphoreType.DMA((count,)),
            pltpu.SemaphoreType.DMA((count,)),
            pltpu.SemaphoreType.DMA((3,)),
            pltpu.SemaphoreType.DMA((3,)),
        ],
        compiler_params=pltpu.CompilerParams(
            collective_id=0, has_side_effects=True, vmem_limit_bytes=20 * MIB
        ),
        cost_estimate=pl.CostEstimate(
            flops=8 * first.shape[0] * cell_count * cell_count,
            bytes_accessed=8 * cell_count * cell_count,
            transcendentals=0,
        ),
    )(
        cells,
        inner_table,
        cross_table,
        pack,
    )


def attention_kernel(
    scale,
    query_ref,
    grad_ref,
    key_ref,
    value_ref,
    cell_code_ref,
    anchor_code_ref,
    dead_ref,
    attended_ref,
    grad_query_ref,
    grad_key_ref,
    grad_value_ref,
):
    anchors = key_ref.shape[0]
    half = key_ref.shape[1] // 2
    left = lax.broadcasted_iota(jnp.int32, key_ref.shape, 1) < half

    def both(ref):
        rows = ref[...]
        none = jnp.zeros_like(rows)
        return jnp.concatenate([jnp.where(left, rows, none), jnp.where(left, none, rows)], axis=0)

    keys, values = both(key_ref), both(value_ref)
    queries, grads = query_ref[...], grad_ref[...]
    scores = contract(queries, keys, 1, 1)
    grad_prob = contract(grads, values, 1, 1)
    bias = cell_code_ref[...] * anchor_code_ref[...] + dead_ref[...]
    lows, grad_lows = [], []
    for head in range(2):
        part = slice(head * anchors, (head + 1) * anchors)
        score = scores[:, part] * scale + bias
        exp_scores = jnp.exp(score - jnp.max(score, axis=1, keepdims=True))
        weights = exp_scores * (1.0 / jnp.sum(exp_scores, axis=1, keepdims=True))
        low = weights.astype(jnp.bfloat16)
        gradient = grad_prob[:, part]
        dots = jnp.sum(low.astype(jnp.float32) * gradient, axis=1, keepdims=True)
        lows.append(low)
        grad_lows.append((weights * (gradient - dots)).astype(jnp.bfloat16))
    low = jnp.concatenate(lows, axis=1)
    grad_low = jnp.concatenate(grad_lows, axis=1)
    attended_ref[...] = contract(low, values, 1, 0).astype(jnp.bfloat16)
    grad_query_ref[...] = (contract(grad_low, keys, 1, 0) * scale).astype(jnp.bfloat16)
    upper = lax.broadcasted_iota(jnp.int32, grad_key_ref.shape, 0) < half
    grad_key = contract(queries, grad_low, 0, 0) * scale
    grad_key_ref[...] = jnp.where(upper, grad_key[:, :anchors], grad_key[:, anchors:])
    grad_value = contract(grads, low, 0, 0)
    grad_value_ref[...] = jnp.where(upper, grad_value[:, :anchors], grad_value[:, anchors:])


def attention(queries, grads, keyvals, cell_code, anchor_code, dead):
    cells = queries.shape[0]
    anchors = keyvals.shape[0]
    pairs = HEADS // 2
    wide = MODEL_WIDTH // pairs
    rows = pl.BlockSpec((cells, wide), lambda i: (0, i))
    keys = pl.BlockSpec((anchors, wide), lambda i: (0, i))
    values = pl.BlockSpec((anchors, wide), lambda i: (0, i + pairs))
    turned = pl.BlockSpec((wide, anchors), lambda i: (i, 0))
    fixed = lambda shape: pl.BlockSpec(shape, lambda i: (0, 0))
    limit = min(56 * MIB, 8 * MIB + 64 * cells * anchors)
    return pl.pallas_call(
        functools.partial(attention_kernel, 1.0 / math.sqrt(MODEL_WIDTH // HEADS)),
        grid=(pairs,),
        in_specs=[rows, rows, keys, values, fixed((cells, 1)), fixed((1, anchors)), fixed((1, anchors))],
        out_specs=[rows, rows, turned, turned],
        out_shape=(
            jax.ShapeDtypeStruct((cells, MODEL_WIDTH), jnp.bfloat16),
            jax.ShapeDtypeStruct((cells, MODEL_WIDTH), jnp.bfloat16),
            jax.ShapeDtypeStruct((MODEL_WIDTH, anchors), jnp.float32),
            jax.ShapeDtypeStruct((MODEL_WIDTH, anchors), jnp.float32),
        ),
        compiler_params=pltpu.CompilerParams(vmem_limit_bytes=limit),
        cost_estimate=pl.CostEstimate(
            flops=24 * cells * anchors * MODEL_WIDTH,
            bytes_accessed=8 * cells * MODEL_WIDTH,
            transcendentals=cells * anchors * HEADS,
        ),
    )(queries, grads, keyvals, keyvals, cell_code[:, None], anchor_code[None, :], dead[None, :])


def tail_kernel(
    count,
    cotangent_ref,
    attended_ref,
    grad_query_ref,
    normed_ref,
    mixed_ref,
    inverse_ref,
    query_matrix_ref,
    inner_high_ref,
    inner_low_ref,
    cross_map_ref,
    weighted_map_ref,
    grad_key_ref,
    grad_value_ref,
    tokens_ref,
    cell_grads_ref,
    weight_grads_ref,
    query_sum,
    output_sum,
    key_sum,
    value_sum,
    own,
    peer,
    face_send,
    face_recv,
    sum_send,
    sum_recv,
    *buffers,
):
    me = lax.axis_index("blk")
    quarter = count // 4
    rows = 4 * MODEL_WIDTH // count
    slots = own.shape[1]
    stages = quarter.bit_length() - 1
    place = lax.div(me, quarter)
    barrier = pltpu.get_barrier_semaphore()

    def greet(step, carry):
        pl.semaphore_signal(
            barrier, inc=1, device_id={"blk": lax.rem(me + step, count)}, device_id_type=MESH
        )
        return carry

    lax.fori_loop(1, count, greet, 0)

    def upper_bit(bit):
        return lax.rem(lax.div(me, bit), 2)

    def copy(source, target, place_in_sems, bit):
        return pltpu.make_async_remote_copy(
            src_ref=source,
            dst_ref=target,
            send_sem=sum_send.at[place_in_sems],
            recv_sem=sum_recv.at[place_in_sems],
            device_id={"blk": me + bit - 2 * bit * upper_bit(bit)},
            device_id_type=MESH,
        )

    def send(stage, kind, total):
        half = quarter >> (stage + 1)
        bit = 1 << stage
        upper = upper_bit(bit)
        out, into = buffers[8 * stage + 2 * kind], buffers[8 * stage + 2 * kind + 1]
        for i in range(half):
            out[i] = total[2 * i + 1 - upper].astype(jnp.bfloat16)
            total[i] = total[2 * i + upper]
        moved = copy(out, into, 4 * stage + kind, bit)
        moved.start()

        def take():
            moved.wait()
            for i in range(half):
                total[i] = total[i] + into[i].astype(jnp.float32)

        return take

    totals = (output_sum, query_sum, key_sum, value_sum)
    shape = (quarter, rows, MODEL_WIDTH)
    output_sum[...] = contract(cotangent_ref[...], attended_ref[...], 0, 0).reshape(shape)
    key_sum[...] = grad_key_ref[...].reshape(key_sum.shape)
    value_sum[...] = grad_value_ref[...].reshape(value_sum.shape)
    pl.semaphore_wait(barrier, count - 1)
    waits = [send(0, 0, output_sum)]
    query_sum[...] = contract(grad_query_ref[...], normed_ref[...], 0, 0).reshape(shape)
    waits += [send(0, kind, totals[kind]) for kind in range(1, 4)]

    grad_normed = contract(grad_query_ref[...], query_matrix_ref[...], 1, 1)
    inverse = inverse_ref[...]
    normal_hat = mixed_ref[...].astype(jnp.float32) * inverse
    grad_mixed = (
        cotangent_ref[...].astype(jnp.float32)
        + inverse
        * (grad_normed - normal_hat * jnp.mean(grad_normed * normal_hat, axis=1, keepdims=True))
    ).astype(jnp.bfloat16)
    cell_grads_ref[...] = grad_mixed
    chosen = contract(cross_map_ref[...], grad_mixed, 0, 0)
    own[0] = chosen[:slots].astype(jnp.bfloat16)
    own[1] = chosen[slots:].astype(jnp.bfloat16)

    def sent(source, target, number, by):
        return pltpu.make_async_remote_copy(
            src_ref=source,
            dst_ref=target,
            send_sem=face_send.at[number],
            recv_sem=face_recv.at[number],
            device_id={"blk": lax.rem(me + by + count, count)},
            device_id_type=MESH,
        )

    down = sent(own.at[1], peer.at[0], 0, -1)
    up = sent(own.at[0], peer.at[1], 1, 1)

    for stage in range(1, stages):
        following = []
        for kind in range(4):
            waits[kind]()
            following.append(send(stage, kind, totals[kind]))
        waits = following

    @pl.when(me > 0)
    def _():
        down.start()

    @pl.when(me < count - 1)
    def _():
        up.start()

    @pl.when(me == 0)
    def _():
        peer[1] = jnp.zeros(peer.shape[1:], peer.dtype)

    @pl.when(me == count - 1)
    def _():
        peer[0] = jnp.zeros(peer.shape[1:], peer.dtype)

    result = (
        cell_grads_ref[...].astype(jnp.float32)
        + contract(inner_high_ref[...], cell_grads_ref[...], 1, 0)
        + contract(inner_low_ref[...], cell_grads_ref[...], 1, 0)
    )
    for take in waits:
        take()
    wide_out, wide_in, pair_out, pair_in, last_out, last_in, last_pair_out, last_pair_in = buffers[
        8 * stages :
    ]
    odd = lax.rem(place, 2) > 0
    wide_out[...] = jnp.where(odd, query_sum[0], output_sum[0]).astype(jnp.bfloat16)
    pair_out[...] = jnp.where(odd, value_sum[0], key_sum[0]).astype(jnp.bfloat16)
    wide = copy(wide_out, wide_in, 4 * stages, quarter)
    pair = copy(pair_out, pair_in, 4 * stages + 1, quarter)
    wide.start()
    pair.start()
    wide_kept = jnp.where(odd, output_sum[0], query_sum[0])
    pair_kept = jnp.where(odd, key_sum[0], value_sum[0])

    @pl.when(me < count - 1)
    def _():
        down.wait_recv()
        up.wait_send()

    @pl.when(me > 0)
    def _():
        up.wait_recv()
        down.wait_send()

    flux = jnp.concatenate(
        [
            (peer[0].astype(jnp.float32) - own[0].astype(jnp.float32)).astype(jnp.bfloat16),
            (peer[1].astype(jnp.float32) - own[1].astype(jnp.float32)).astype(jnp.bfloat16),
        ],
        axis=0,
    )
    wide.wait()
    pair.wait()
    query_sum[0] = wide_kept + wide_in[...].astype(jnp.float32)
    key_sum[0] = pair_kept + pair_in[...].astype(jnp.float32)
    last = copy(last_out, last_in, 4 * stages + 2, 2 * quarter)
    last_pair = copy(last_pair_out, last_pair_in, 4 * stages + 3, 2 * quarter)
    outer = lax.rem(place + 1, 4) < 2
    inside = lax.rem(place + 1, 4) >= 2

    @pl.when(inside)
    def _():
        last_out[...] = query_sum[0].astype(jnp.bfloat16)
        last.start()

    @pl.when(outer)
    def _():
        last_pair_out[...] = key_sum[0].astype(jnp.bfloat16)
        last_pair.start()

    cell_grads_ref[...] = (result + contract(weighted_map_ref[...], flux, 1, 0)).astype(jnp.bfloat16)

    @pl.when(inside)
    def _():
        last_pair.wait_recv()
        total = key_sum[0] + last_pair_in[...].astype(jnp.float32)
        weight_grads_ref[...] = contract(
            total, tokens_ref[...].astype(jnp.float32), 1, 0, lax.Precision.HIGHEST
        )
        last.wait_send()

    @pl.when(outer)
    def _():
        last.wait_recv()
        weight_grads_ref[...] = query_sum[0] + last_in[...].astype(jnp.float32)
        last_pair.wait_send()


def tail(*operands):
    count = lax.axis_size("blk")
    cells = operands[0].shape
    anchors = operands[-1].shape[0]
    slots = operands[9].shape[1] // 2
    quarter = count // 4
    rows = 4 * MODEL_WIDTH // count
    stages = quarter.bit_length() - 1
    low = lambda *shape: pltpu.VMEM(shape, jnp.bfloat16)
    full = lambda *shape: pltpu.VMEM(shape, jnp.float32)
    buffers = []
    for stage in range(stages):
        half = quarter >> (stage + 1)
        buffers += [low(half, rows, MODEL_WIDTH)] * 4 + [low(half, rows, anchors)] * 4
    buffers += ([low(rows, MODEL_WIDTH)] * 2 + [low(rows, anchors)] * 2) * 2
    vmem = pl.BlockSpec(memory_space=pltpu.VMEM)
    return pl.pallas_call(
        functools.partial(tail_kernel, count),
        in_specs=[vmem] * len(operands),
        out_specs=[vmem] * 2,
        out_shape=(
            jax.ShapeDtypeStruct(cells, jnp.bfloat16),
            jax.ShapeDtypeStruct((rows, MODEL_WIDTH), jnp.float32),
        ),
        scratch_shapes=[
            full(quarter, rows, MODEL_WIDTH),
            full(quarter, rows, MODEL_WIDTH),
            full(quarter, rows, anchors),
            full(quarter, rows, anchors),
            low(2, slots, MODEL_WIDTH),
            low(2, slots, MODEL_WIDTH),
            pltpu.SemaphoreType.DMA((2,)),
            pltpu.SemaphoreType.DMA((2,)),
            pltpu.SemaphoreType.DMA((4 * stages + 4,)),
            pltpu.SemaphoreType.DMA((4 * stages + 4,)),
        ]
        + buffers,
        compiler_params=pltpu.CompilerParams(
            collective_id=1, has_side_effects=True, vmem_limit_bytes=48 * MIB
        ),
    )(*operands)


def shards(
    cell_features,
    cell_geometry_rows,
    anchor_token_features,
    anchor_geometry_rows,
    live_anchor_count,
    inner_face_first,
    inner_face_second,
    inner_face_weight,
    upper_face_cell,
    lower_face_cell,
    upper_face_weight,
    upper_slot_count,
    query_matrix,
    anchor_keyvalue_matrix,
    output_matrix,
    cotangent,
):
    own_anchors = anchor_token_features.shape[0]
    slot_index = jnp.arange(upper_face_cell.shape[0], dtype=jnp.int32)
    live_weight = jnp.where(
        slot_index < upper_slot_count[0], upper_face_weight.astype(jnp.float32), 0.0
    )
    live = jnp.arange(own_anchors, dtype=jnp.int32) < live_anchor_count[0]
    side = jnp.concatenate([anchor_geometry_rows, live.astype(jnp.bfloat16)])
    half_width = MODEL_WIDTH // 2
    pack = jnp.concatenate(
        [
            anchor_token_features.reshape(2 * own_anchors, half_width),
            jnp.broadcast_to(side[:, None], (2 * own_anchors, 128)),
        ],
        axis=1,
    )
    mixed_rows, normed, inverse_rms, inner_high, inner_low, cross_map, weighted_map, packed = front(
        cell_features,
        inner_face_first,
        inner_face_second,
        inner_face_weight,
        jnp.concatenate([upper_face_cell, lower_face_cell]),
        live_weight,
        pack,
    )
    tokens = packed[:, :, :half_width].reshape(-1, MODEL_WIDTH)
    anchor_code = packed[:, :own_anchors, half_width].reshape(-1).astype(jnp.float32)
    dead = jnp.where(packed[:, own_anchors:, half_width] > 0, 0.0, -jnp.inf)
    dead = dead.reshape(-1).astype(jnp.float32)
    queries = contract(normed, query_matrix, 1, 0).astype(jnp.bfloat16)
    keyvals = contract(tokens, anchor_keyvalue_matrix, 1, 0).astype(jnp.bfloat16)
    attended_gradient = contract(cotangent, output_matrix, 1, 1).astype(jnp.bfloat16)
    attended, grad_queries, grad_keys, grad_values = attention(
        queries, attended_gradient, keyvals, cell_geometry_rows, anchor_code, dead
    )
    cell_grads, weight_grads = tail(
        cotangent,
        attended,
        grad_queries,
        normed,
        mixed_rows,
        inverse_rms,
        query_matrix,
        inner_high,
        inner_low,
        cross_map,
        weighted_map,
        grad_keys,
        grad_values,
        tokens,
    )
    layer_output = (
        mixed_rows.astype(jnp.float32) + contract(attended, output_matrix, 1, 0)
    ).astype(jnp.bfloat16)
    return (layer_output, cell_grads, weight_grads)


def solution(mesh):
    cells = P(("groups", "blk"))
    in_specs = (cells,) * 12 + (P(), P(), P(), cells)
    return jax.shard_map(
        shards, mesh=mesh, in_specs=in_specs, out_specs=(cells, cells, cells), check_vma=False
    )
```

```python
import functools
import math

import jax
import jax.numpy as jnp
from jax import lax
from jax.experimental import pallas as pl
from jax.experimental.pallas import tpu as pltpu
from jax.sharding import PartitionSpec as P

MODEL_WIDTH = 768
HEADS = 12
EPS = 1e-06
MIB = 1 << 20
MESH = pl.DeviceIdType.MESH


def contract(left, right, left_dim, right_dim, precision=None):
    return lax.dot_general(
        left,
        right,
        (((left_dim,), (right_dim,)), ((), ())),
        precision=precision,
        preferred_element_type=jnp.float32,
    )


def exchanged(shard, bit):
    count = lax.axis_size("blk")
    return lax.ppermute(shard, "blk", [(i, i ^ bit) for i in range(count)])


def passed_along(shard, by):
    count = lax.axis_size("blk")
    return lax.ppermute(
        shard, "blk", [(i, i + by) for i in range(count) if 0 <= i + by < count]
    )


def front_kernel(
    count,
    cells_ref,
    inner_ref,
    cross_ref,
    pack_ref,
    cotangent_ref,
    query_matrix_ref,
    output_matrix_ref,
    mixed_ref,
    normed_ref,
    inverse_ref,
    inner_high_ref,
    inner_low_ref,
    cross_map_ref,
    weighted_map_ref,
    gathered_ref,
    queries_ref,
    grads_ref,
    own,
    peer,
    lower_live,
    landed,
    pack_send,
    pack_recv,
    face_send,
    face_recv,
):
    me = lax.axis_index("blk")
    slots = cross_ref.shape[1]
    live_ref = cross_ref
    cell_count = cells_ref.shape[0]
    barrier = pltpu.get_barrier_semaphore()

    def greet(step, carry):
        pl.semaphore_signal(
            barrier, inc=1, device_id={"blk": lax.rem(me + step, count)}, device_id_type=MESH
        )
        return carry

    lax.fori_loop(1, count, greet, 0)
    ids = lax.broadcasted_iota(jnp.int32, (cell_count, 2 * slots), 0)
    cross_map = jnp.where(
        ids
        == jnp.concatenate([cross_ref[...][:1], cross_ref[...][1:2]], axis=1).astype(jnp.int32),
        1.0,
        0.0,
    )
    cross_map_ref[...] = cross_map.astype(jnp.bfloat16)
    rows = cells_ref[...]
    chosen = contract(cross_map_ref[...], rows, 0, 0)
    own[0] = chosen[:slots].astype(jnp.bfloat16)
    own[1] = chosen[slots:].astype(jnp.bfloat16)
    pl.semaphore_wait(barrier, count - 1)

    def sent(source, target, place, by):
        return pltpu.make_async_remote_copy(
            src_ref=source,
            dst_ref=target,
            send_sem=face_send.at[place],
            recv_sem=face_recv.at[place],
            device_id={"blk": lax.rem(me + by + count, count)},
            device_id_type=MESH,
        )

    down = sent(own.at[1], peer.at[0], 0, -1)
    up = sent(own.at[0], peer.at[1], 1, 1)
    weights = sent(live_ref, lower_live, 2, 1)

    @pl.when(me > 0)
    def _():
        down.start()

    @pl.when(me < count - 1)
    def _():
        up.start()
        weights.start()

    def pack_copy(step, place):
        return pltpu.make_async_remote_copy(
            src_ref=pack_ref,
            dst_ref=landed.at[place],
            send_sem=pack_send.at[step],
            recv_sem=pack_recv.at[place],
            device_id={"blk": lax.rem(me + step, count)},
            device_id_type=MESH,
        )

    def send_pack(step, carry):
        pack_copy(step, me).start()
        return carry

    lax.fori_loop(1, count, send_pack, 0)
    landed[me] = pack_ref[...]

    @pl.when(me == 0)
    def _():
        peer[1] = jnp.zeros(peer.shape[1:], peer.dtype)
        lower_live[...] = jnp.zeros_like(lower_live)

    @pl.when(me == count - 1)
    def _():
        peer[0] = jnp.zeros(peer.shape[1:], peer.dtype)

    inner_rows = inner_ref[...]
    first, second = inner_rows[:1].astype(jnp.int32), inner_rows[1:2].astype(jnp.int32)
    weight = inner_rows[2:3]
    weight_high = weight.astype(jnp.bfloat16).astype(jnp.float32)
    weight_low = weight - weight_high
    ids = lax.broadcasted_iota(jnp.int32, (cell_count, inner_ref.shape[1]), 0)
    difference = jnp.where(ids == second, 1.0, 0.0) - jnp.where(ids == first, 1.0, 0.0)
    low = difference.astype(jnp.bfloat16)
    total = contract((difference * weight_high).astype(jnp.bfloat16), low, 1, 1)
    total = total + contract((difference * weight_low).astype(jnp.bfloat16), low, 1, 1)
    high_part = (-total).astype(jnp.bfloat16)
    inner_high_ref[...] = high_part
    inner_low_ref[...] = (-total - high_part.astype(jnp.float32)).astype(jnp.bfloat16)
    inner = contract(inner_high_ref[...], rows, 1, 0) + contract(inner_low_ref[...], rows, 1, 0)
    grads_ref[...] = contract(cotangent_ref[...], output_matrix_ref[...], 1, 1).astype(jnp.bfloat16)

    @pl.when(me < count - 1)
    def _():
        down.wait_recv()
        up.wait_send()
        weights.wait_send()

    @pl.when(me > 0)
    def _():
        up.wait_recv()
        weights.wait_recv()
        down.wait_send()

    live = jnp.concatenate(
        [cross_ref[...][2:3], lower_live[...][2:3]], axis=1
    )
    weighted_map_ref[...] = (cross_map_ref[...].astype(jnp.float32) * live).astype(jnp.bfloat16)
    flux = jnp.concatenate(
        [
            (peer[0].astype(jnp.float32) - own[0].astype(jnp.float32)).astype(jnp.bfloat16),
            (peer[1].astype(jnp.float32) - own[1].astype(jnp.float32)).astype(jnp.bfloat16),
        ],
        axis=0,
    )
    mixed = (
        rows.astype(jnp.float32) + inner + contract(weighted_map_ref[...], flux, 1, 0)
    ).astype(jnp.bfloat16)
    mixed_ref[...] = mixed
    mixed = mixed.astype(jnp.float32)
    inverse = lax.rsqrt(jnp.mean(mixed * mixed, axis=1, keepdims=True) + EPS)
    inverse_ref[...] = inverse
    normed_ref[...] = (mixed * inverse).astype(jnp.bfloat16)
    queries_ref[...] = contract(normed_ref[...], query_matrix_ref[...], 1, 0).astype(jnp.bfloat16)

    def take_pack(step, carry):
        pack_copy(step, lax.rem(me + count - step, count)).wait_recv()
        pack_copy(step, me).wait_send()
        return carry

    lax.fori_loop(1, count, take_pack, 0)
    gathered_ref[...] = landed[...]


def front(
    cells, first, second, weight, upper_cells, lower_cells, live, pack, cotangent, query_matrix, output_matrix
):
    count = lax.axis_size("blk")
    cell_count = cells.shape[0]
    slots = live.shape[0]
    line = lax.broadcasted_iota(jnp.int32, (8, 1), 0)
    table = lambda one, two, three: jnp.where(
        line == 0,
        one.astype(jnp.float32)[None, :],
        jnp.where(line == 1, two.astype(jnp.float32)[None, :], three[None, :]),
    )
    inner_table = table(first, second, weight)
    cross_table = table(upper_cells, lower_cells, live)
    low_type = lambda *shape: jax.ShapeDtypeStruct(shape, jnp.bfloat16)
    return pl.pallas_call(
        functools.partial(front_kernel, count),
        in_specs=[pl.BlockSpec(memory_space=pltpu.VMEM)] * 7,
        out_specs=[pl.BlockSpec(memory_space=pltpu.VMEM)] * 10,
        out_shape=(
            low_type(*cells.shape),
            low_type(*cells.shape),
            jax.ShapeDtypeStruct((cell_count, 1), jnp.float32),
            low_type(cell_count, cell_count),
            low_type(cell_count, cell_count),
            low_type(cell_count, 2 * slots),
            low_type(cell_count, 2 * slots),
            low_type(count, *pack.shape),
            low_type(*cells.shape),
            low_type(*cells.shape),
        ),
        scratch_shapes=[
            pltpu.VMEM((2, slots, cells.shape[1]), jnp.bfloat16),
            pltpu.VMEM((2, slots, cells.shape[1]), jnp.bfloat16),
            pltpu.VMEM((8, slots), jnp.float32),
            pltpu.VMEM((count, *pack.shape), jnp.bfloat16),
            pltpu.SemaphoreType.DMA((count,)),
            pltpu.SemaphoreType.DMA((count,)),
            pltpu.SemaphoreType.DMA((3,)),
            pltpu.SemaphoreType.DMA((3,)),
        ],
        compiler_params=pltpu.CompilerParams(
            collective_id=0, has_side_effects=True, vmem_limit_bytes=(20 if count <= 32 else 28) * MIB
        ),
        cost_estimate=pl.CostEstimate(
            flops=8 * first.shape[0] * cell_count * cell_count,
            bytes_accessed=8 * cell_count * cell_count,
            transcendentals=0,
        ),
    )(
        cells,
        inner_table,
        cross_table,
        pack,
        cotangent,
        query_matrix,
        output_matrix,
    )


def attention_kernel(
    scale,
    query_ref,
    grad_ref,
    key_ref,
    value_ref,
    cell_code_ref,
    anchor_code_ref,
    dead_ref,
    attended_ref,
    grad_query_ref,
    grad_key_ref,
    grad_value_ref,
):
    anchors = key_ref.shape[0]
    half = key_ref.shape[1] // 2
    left = lax.broadcasted_iota(jnp.int32, key_ref.shape, 1) < half

    def both(ref):
        rows = ref[...]
        none = jnp.zeros_like(rows)
        return jnp.concatenate([jnp.where(left, rows, none), jnp.where(left, none, rows)], axis=0)

    keys, values = both(key_ref), both(value_ref)
    queries, grads = query_ref[...], grad_ref[...]
    scores = contract(queries, keys, 1, 1)
    grad_prob = contract(grads, values, 1, 1)
    bias = cell_code_ref[...] * anchor_code_ref[...] + dead_ref[...]
    lows, grad_lows = [], []
    for head in range(2):
        part = slice(head * anchors, (head + 1) * anchors)
        score = scores[:, part] * scale + bias
        exp_scores = jnp.exp(score - jnp.max(score, axis=1, keepdims=True))
        weights = exp_scores * (1.0 / jnp.sum(exp_scores, axis=1, keepdims=True))
        low = weights.astype(jnp.bfloat16)
        gradient = grad_prob[:, part]
        dots = jnp.sum(low.astype(jnp.float32) * gradient, axis=1, keepdims=True)
        lows.append(low)
        grad_lows.append((weights * (gradient - dots)).astype(jnp.bfloat16))
    low = jnp.concatenate(lows, axis=1)
    grad_low = jnp.concatenate(grad_lows, axis=1)
    attended_ref[...] = contract(low, values, 1, 0).astype(jnp.bfloat16)
    grad_query_ref[...] = (contract(grad_low, keys, 1, 0) * scale).astype(jnp.bfloat16)
    upper = lax.broadcasted_iota(jnp.int32, grad_key_ref.shape, 0) < half
    grad_key = contract(queries, grad_low, 0, 0) * scale
    grad_key_ref[...] = jnp.where(upper, grad_key[:, :anchors], grad_key[:, anchors:])
    grad_value = contract(grads, low, 0, 0)
    grad_value_ref[...] = jnp.where(upper, grad_value[:, :anchors], grad_value[:, anchors:])


def attention(queries, grads, keyvals, cell_code, anchor_code, dead):
    cells = queries.shape[0]
    anchors = keyvals.shape[0]
    pairs = HEADS // 2
    wide = MODEL_WIDTH // pairs
    rows = pl.BlockSpec((cells, wide), lambda i: (0, i))
    keys = pl.BlockSpec((anchors, wide), lambda i: (0, i))
    values = pl.BlockSpec((anchors, wide), lambda i: (0, i + pairs))
    turned = pl.BlockSpec((wide, anchors), lambda i: (i, 0))
    fixed = lambda shape: pl.BlockSpec(shape, lambda i: (0, 0))
    limit = min(56 * MIB, 8 * MIB + 64 * cells * anchors)
    return pl.pallas_call(
        functools.partial(attention_kernel, 1.0 / math.sqrt(MODEL_WIDTH // HEADS)),
        grid=(pairs,),
        in_specs=[rows, rows, keys, values, fixed((cells, 1)), fixed((1, anchors)), fixed((1, anchors))],
        out_specs=[rows, rows, turned, turned],
        out_shape=(
            jax.ShapeDtypeStruct((cells, MODEL_WIDTH), jnp.bfloat16),
            jax.ShapeDtypeStruct((cells, MODEL_WIDTH), jnp.bfloat16),
            jax.ShapeDtypeStruct((MODEL_WIDTH, anchors), jnp.float32),
            jax.ShapeDtypeStruct((MODEL_WIDTH, anchors), jnp.float32),
        ),
        compiler_params=pltpu.CompilerParams(vmem_limit_bytes=limit),
        cost_estimate=pl.CostEstimate(
            flops=24 * cells * anchors * MODEL_WIDTH,
            bytes_accessed=8 * cells * MODEL_WIDTH,
            transcendentals=cells * anchors * HEADS,
        ),
    )(queries, grads, keyvals, keyvals, cell_code[:, None], anchor_code[None, :], dead[None, :])


def tail_kernel(
    count,
    cotangent_ref,
    attended_ref,
    grad_query_ref,
    normed_ref,
    mixed_ref,
    inverse_ref,
    query_matrix_ref,
    inner_high_ref,
    inner_low_ref,
    cross_map_ref,
    weighted_map_ref,
    grad_key_ref,
    grad_value_ref,
    output_matrix_ref,
    tokens_ref,
    layer_output_ref,
    cell_grads_ref,
    weight_grads_ref,
    query_sum,
    output_sum,
    key_sum,
    value_sum,
    own,
    peer,
    face_send,
    face_recv,
    sum_send,
    sum_recv,
    *buffers,
):
    me = lax.axis_index("blk")
    quarter = count // 4
    rows = 4 * MODEL_WIDTH // count
    slots = own.shape[1]
    stages = quarter.bit_length() - 1
    place = lax.div(me, quarter)
    barrier = pltpu.get_barrier_semaphore()

    def greet(step, carry):
        pl.semaphore_signal(
            barrier, inc=1, device_id={"blk": lax.rem(me + step, count)}, device_id_type=MESH
        )
        return carry

    lax.fori_loop(1, count, greet, 0)

    def upper_bit(bit):
        return lax.rem(lax.div(me, bit), 2)

    def copy(source, target, place_in_sems, bit):
        return pltpu.make_async_remote_copy(
            src_ref=source,
            dst_ref=target,
            send_sem=sum_send.at[place_in_sems],
            recv_sem=sum_recv.at[place_in_sems],
            device_id={"blk": me + bit - 2 * bit * upper_bit(bit)},
            device_id_type=MESH,
        )

    def send(stage, kind, total):
        half = quarter >> (stage + 1)
        bit = 1 << stage
        upper = upper_bit(bit)
        out, into = buffers[8 * stage + 2 * kind], buffers[8 * stage + 2 * kind + 1]
        for i in range(half):
            out[i] = total[2 * i + 1 - upper].astype(jnp.bfloat16)
            total[i] = total[2 * i + upper]
        moved = copy(out, into, 4 * stage + kind, bit)
        moved.start()

        def take():
            moved.wait()
            for i in range(half):
                total[i] = total[i] + into[i].astype(jnp.float32)

        return take

    totals = (output_sum, query_sum, key_sum, value_sum)
    shape = (quarter, rows, MODEL_WIDTH)
    output_sum[...] = contract(cotangent_ref[...], attended_ref[...], 0, 0).reshape(shape)
    key_sum[...] = grad_key_ref[...].reshape(key_sum.shape)
    value_sum[...] = grad_value_ref[...].reshape(value_sum.shape)
    pl.semaphore_wait(barrier, count - 1)
    waits = [send(0, 0, output_sum)]
    query_sum[...] = contract(grad_query_ref[...], normed_ref[...], 0, 0).reshape(shape)
    waits += [send(0, kind, totals[kind]) for kind in range(1, 4)]

    grad_normed = contract(grad_query_ref[...], query_matrix_ref[...], 1, 1)
    for stage in range(1, stages):
        following = []
        for kind in range(4):
            waits[kind]()
            following.append(send(stage, kind, totals[kind]))
        waits = following

    inverse = inverse_ref[...]
    normal_hat = mixed_ref[...].astype(jnp.float32) * inverse
    grad_mixed = (
        cotangent_ref[...].astype(jnp.float32)
        + inverse
        * (grad_normed - normal_hat * jnp.mean(grad_normed * normal_hat, axis=1, keepdims=True))
    ).astype(jnp.bfloat16)
    cell_grads_ref[...] = grad_mixed
    chosen = contract(cross_map_ref[...], grad_mixed, 0, 0)
    own[0] = chosen[:slots].astype(jnp.bfloat16)
    own[1] = chosen[slots:].astype(jnp.bfloat16)

    def sent(source, target, number, by):
        return pltpu.make_async_remote_copy(
            src_ref=source,
            dst_ref=target,
            send_sem=face_send.at[number],
            recv_sem=face_recv.at[number],
            device_id={"blk": lax.rem(me + by + count, count)},
            device_id_type=MESH,
        )

    down = sent(own.at[1], peer.at[0], 0, -1)
    up = sent(own.at[0], peer.at[1], 1, 1)

    @pl.when(me > 0)
    def _():
        down.start()

    @pl.when(me < count - 1)
    def _():
        up.start()

    @pl.when(me == 0)
    def _():
        peer[1] = jnp.zeros(peer.shape[1:], peer.dtype)

    @pl.when(me == count - 1)
    def _():
        peer[0] = jnp.zeros(peer.shape[1:], peer.dtype)

    result = (
        cell_grads_ref[...].astype(jnp.float32)
        + contract(inner_high_ref[...], cell_grads_ref[...], 1, 0)
        + contract(inner_low_ref[...], cell_grads_ref[...], 1, 0)
    )
    layer_output_ref[...] = (
        mixed_ref[...].astype(jnp.float32)
        + contract(attended_ref[...], output_matrix_ref[...], 1, 0)
    ).astype(jnp.bfloat16)
    for take in waits:
        take()
    wide_out, wide_in, pair_out, pair_in, last_out, last_in, last_pair_out, last_pair_in = buffers[
        8 * stages :
    ]
    odd = lax.rem(place, 2) > 0
    wide_out[...] = jnp.where(odd, query_sum[0], output_sum[0]).astype(jnp.bfloat16)
    pair_out[...] = jnp.where(odd, value_sum[0], key_sum[0]).astype(jnp.bfloat16)
    wide = copy(wide_out, wide_in, 4 * stages, quarter)
    pair = copy(pair_out, pair_in, 4 * stages + 1, quarter)
    wide.start()
    pair.start()
    wide_kept = jnp.where(odd, output_sum[0], query_sum[0])
    pair_kept = jnp.where(odd, key_sum[0], value_sum[0])

    @pl.when(me < count - 1)
    def _():
        down.wait_recv()
        up.wait_send()

    @pl.when(me > 0)
    def _():
        up.wait_recv()
        down.wait_send()

    flux = jnp.concatenate(
        [
            (peer[0].astype(jnp.float32) - own[0].astype(jnp.float32)).astype(jnp.bfloat16),
            (peer[1].astype(jnp.float32) - own[1].astype(jnp.float32)).astype(jnp.bfloat16),
        ],
        axis=0,
    )
    wide.wait()
    pair.wait()
    query_sum[0] = wide_kept + wide_in[...].astype(jnp.float32)
    key_sum[0] = pair_kept + pair_in[...].astype(jnp.float32)
    last = copy(last_out, last_in, 4 * stages + 2, 2 * quarter)
    last_pair = copy(last_pair_out, last_pair_in, 4 * stages + 3, 2 * quarter)
    outer = lax.rem(place + 1, 4) < 2
    inside = lax.rem(place + 1, 4) >= 2

    @pl.when(inside)
    def _():
        last_out[...] = query_sum[0].astype(jnp.bfloat16)
        last.start()

    @pl.when(outer)
    def _():
        last_pair_out[...] = key_sum[0].astype(jnp.bfloat16)
        last_pair.start()

    cell_grads_ref[...] = (result + contract(weighted_map_ref[...], flux, 1, 0)).astype(jnp.bfloat16)

    @pl.when(inside)
    def _():
        last_pair.wait_recv()
        total = key_sum[0] + last_pair_in[...].astype(jnp.float32)
        weight_grads_ref[...] = contract(
            total, tokens_ref[...].astype(jnp.float32), 1, 0, lax.Precision.HIGHEST
        )
        last.wait_send()

    @pl.when(outer)
    def _():
        last.wait_recv()
        weight_grads_ref[...] = query_sum[0] + last_in[...].astype(jnp.float32)
        last_pair.wait_send()


def tail(*operands):
    count = lax.axis_size("blk")
    cells = operands[0].shape
    anchors = operands[-1].shape[0]
    slots = operands[9].shape[1] // 2
    quarter = count // 4
    rows = 4 * MODEL_WIDTH // count
    stages = quarter.bit_length() - 1
    low = lambda *shape: pltpu.VMEM(shape, jnp.bfloat16)
    full = lambda *shape: pltpu.VMEM(shape, jnp.float32)
    buffers = []
    for stage in range(stages):
        half = quarter >> (stage + 1)
        buffers += [low(half, rows, MODEL_WIDTH)] * 4 + [low(half, rows, anchors)] * 4
    buffers += ([low(rows, MODEL_WIDTH)] * 2 + [low(rows, anchors)] * 2) * 2
    vmem = pl.BlockSpec(memory_space=pltpu.VMEM)
    return pl.pallas_call(
        functools.partial(tail_kernel, count),
        in_specs=[vmem] * len(operands),
        out_specs=[vmem] * 3,
        out_shape=(
            jax.ShapeDtypeStruct(cells, jnp.bfloat16),
            jax.ShapeDtypeStruct(cells, jnp.bfloat16),
            jax.ShapeDtypeStruct((rows, MODEL_WIDTH), jnp.float32),
        ),
        scratch_shapes=[
            full(quarter, rows, MODEL_WIDTH),
            full(quarter, rows, MODEL_WIDTH),
            full(quarter, rows, anchors),
            full(quarter, rows, anchors),
            low(2, slots, MODEL_WIDTH),
            low(2, slots, MODEL_WIDTH),
            pltpu.SemaphoreType.DMA((2,)),
            pltpu.SemaphoreType.DMA((2,)),
            pltpu.SemaphoreType.DMA((4 * stages + 4,)),
            pltpu.SemaphoreType.DMA((4 * stages + 4,)),
        ]
        + buffers,
        compiler_params=pltpu.CompilerParams(
            collective_id=1, has_side_effects=True, vmem_limit_bytes=(24 if count <= 32 else 44) * MIB
        ),
    )(*operands)


def shards(
    cell_features,
    cell_geometry_rows,
    anchor_token_features,
    anchor_geometry_rows,
    live_anchor_count,
    inner_face_first,
    inner_face_second,
    inner_face_weight,
    upper_face_cell,
    lower_face_cell,
    upper_face_weight,
    upper_slot_count,
    query_matrix,
    anchor_keyvalue_matrix,
    output_matrix,
    cotangent,
):
    own_anchors = anchor_token_features.shape[0]
    slot_index = jnp.arange(upper_face_cell.shape[0], dtype=jnp.int32)
    live_weight = jnp.where(
        slot_index < upper_slot_count[0], upper_face_weight.astype(jnp.float32), 0.0
    )
    live = jnp.arange(own_anchors, dtype=jnp.int32) < live_anchor_count[0]
    side = jnp.concatenate([anchor_geometry_rows, live.astype(jnp.bfloat16)])
    half_width = MODEL_WIDTH // 2
    pack = jnp.concatenate(
        [
            anchor_token_features.reshape(2 * own_anchors, half_width),
            jnp.broadcast_to(side[:, None], (2 * own_anchors, 128)),
        ],
        axis=1,
    )
    (
        mixed_rows,
        normed,
        inverse_rms,
        inner_high,
        inner_low,
        cross_map,
        weighted_map,
        packed,
        queries,
        attended_gradient,
    ) = front(
        cell_features,
        inner_face_first,
        inner_face_second,
        inner_face_weight,
        upper_face_cell,
        lower_face_cell,
        live_weight,
        pack,
        cotangent,
        query_matrix,
        output_matrix,
    )
    tokens = packed[:, :, :half_width].reshape(-1, MODEL_WIDTH)
    anchor_code = packed[:, :own_anchors, half_width].reshape(-1).astype(jnp.float32)
    dead = jnp.where(packed[:, own_anchors:, half_width] > 0, 0.0, -jnp.inf)
    dead = dead.reshape(-1).astype(jnp.float32)
    keyvals = contract(tokens, anchor_keyvalue_matrix, 1, 0).astype(jnp.bfloat16)
    attended, grad_queries, grad_keys, grad_values = attention(
        queries, attended_gradient, keyvals, cell_geometry_rows, anchor_code, dead
    )
    layer_output, cell_grads, weight_grads = tail(
        cotangent,
        attended,
        grad_queries,
        normed,
        mixed_rows,
        inverse_rms,
        query_matrix,
        inner_high,
        inner_low,
        cross_map,
        weighted_map,
        grad_keys,
        grad_values,
        output_matrix,
        tokens,
    )
    return (layer_output, cell_grads, weight_grads)


def solution(mesh):
    cells = P(("groups", "blk"))
    in_specs = (cells,) * 12 + (P(), P(), P(), cells)
    return jax.shard_map(
        shards, mesh=mesh, in_specs=in_specs, out_specs=(cells, cells, cells), check_vma=False
    )
```

```python
import functools
import math

import jax
import jax.numpy as jnp
from jax import lax
from jax.experimental import pallas as pl
from jax.experimental.pallas import tpu as pltpu
from jax.sharding import PartitionSpec as P

MODEL_WIDTH = 768
HEADS = 12
EPS = 1e-06
MIB = 1 << 20
MESH = pl.DeviceIdType.MESH


def contract(left, right, left_dim, right_dim, precision=None):
    return lax.dot_general(
        left,
        right,
        (((left_dim,), (right_dim,)), ((), ())),
        precision=precision,
        preferred_element_type=jnp.float32,
    )


def exchanged(shard, bit):
    count = lax.axis_size("blk")
    return lax.ppermute(shard, "blk", [(i, i ^ bit) for i in range(count)])


def passed_along(shard, by):
    count = lax.axis_size("blk")
    return lax.ppermute(
        shard, "blk", [(i, i + by) for i in range(count) if 0 <= i + by < count]
    )


def front_kernel(
    count,
    cells_ref,
    inner_ref,
    weight_ref,
    cross_ref,
    live_ref,
    pack_ref,
    cotangent_ref,
    query_matrix_ref,
    output_matrix_ref,
    mixed_ref,
    normed_ref,
    inverse_ref,
    inner_high_ref,
    inner_low_ref,
    cross_map_ref,
    weighted_map_ref,
    gathered_ref,
    queries_ref,
    grads_ref,
    own,
    peer,
    lower_live,
    landed,
    pack_send,
    pack_recv,
    face_send,
    face_recv,
):
    me = lax.axis_index("blk")
    slots = cross_ref.shape[1]
    cell_count = cells_ref.shape[0]
    barrier = pltpu.get_barrier_semaphore()

    def greet(step, carry):
        pl.semaphore_signal(
            barrier, inc=1, device_id={"blk": lax.rem(me + step, count)}, device_id_type=MESH
        )
        return carry

    lax.fori_loop(1, count, greet, 0)
    ids = lax.broadcasted_iota(jnp.int32, (cell_count, 2 * slots), 0)
    cross_map = jnp.where(
        ids
        == jnp.concatenate([cross_ref[...][:1], cross_ref[...][1:2]], axis=1),
        1.0,
        0.0,
    )
    cross_map_ref[...] = cross_map.astype(jnp.bfloat16)
    rows = cells_ref[...]
    chosen = contract(cross_map_ref[...], rows, 0, 0)
    own[0] = chosen[:slots].astype(jnp.bfloat16)
    own[1] = chosen[slots:].astype(jnp.bfloat16)
    pl.semaphore_wait(barrier, count - 1)

    def sent(source, target, place, by):
        return pltpu.make_async_remote_copy(
            src_ref=source,
            dst_ref=target,
            send_sem=face_send.at[place],
            recv_sem=face_recv.at[place],
            device_id={"blk": lax.rem(me + by + count, count)},
            device_id_type=MESH,
        )

    down = sent(own.at[1], peer.at[0], 0, -1)
    up = sent(own.at[0], peer.at[1], 1, 1)
    weights = sent(live_ref, lower_live, 2, 1)

    @pl.when(me > 0)
    def _():
        down.start()

    @pl.when(me < count - 1)
    def _():
        up.start()
        weights.start()

    def pack_copy(step, place):
        return pltpu.make_async_remote_copy(
            src_ref=pack_ref,
            dst_ref=landed.at[place],
            send_sem=pack_send.at[step],
            recv_sem=pack_recv.at[place],
            device_id={"blk": lax.rem(me + step, count)},
            device_id_type=MESH,
        )

    def send_pack(step, carry):
        pack_copy(step, me).start()
        return carry

    lax.fori_loop(1, count, send_pack, 0)
    landed[me] = pack_ref[...]

    @pl.when(me == 0)
    def _():
        peer[1] = jnp.zeros(peer.shape[1:], peer.dtype)
        lower_live[...] = jnp.zeros_like(lower_live)

    @pl.when(me == count - 1)
    def _():
        peer[0] = jnp.zeros(peer.shape[1:], peer.dtype)

    inner_rows = inner_ref[...]
    first, second = inner_rows[:1], inner_rows[1:2]
    weight = weight_ref[...]
    weight_high = weight.astype(jnp.bfloat16).astype(jnp.float32)
    weight_low = weight - weight_high
    ids = lax.broadcasted_iota(jnp.int32, (cell_count, inner_ref.shape[1]), 0)
    difference = jnp.where(ids == second, 1.0, 0.0) - jnp.where(ids == first, 1.0, 0.0)
    low = difference.astype(jnp.bfloat16)
    total = contract((difference * weight_high).astype(jnp.bfloat16), low, 1, 1)
    total = total + contract((difference * weight_low).astype(jnp.bfloat16), low, 1, 1)
    high_part = (-total).astype(jnp.bfloat16)
    inner_high_ref[...] = high_part
    inner_low_ref[...] = (-total - high_part.astype(jnp.float32)).astype(jnp.bfloat16)
    inner = contract(inner_high_ref[...], rows, 1, 0) + contract(inner_low_ref[...], rows, 1, 0)
    grads_ref[...] = contract(cotangent_ref[...], output_matrix_ref[...], 1, 1).astype(jnp.bfloat16)

    @pl.when(me < count - 1)
    def _():
        down.wait_recv()
        up.wait_send()
        weights.wait_send()

    @pl.when(me > 0)
    def _():
        up.wait_recv()
        weights.wait_recv()
        down.wait_send()

    live = jnp.concatenate(
        [live_ref[...][:1], lower_live[...][:1]], axis=1
    )
    weighted_map_ref[...] = (cross_map_ref[...].astype(jnp.float32) * live).astype(jnp.bfloat16)
    flux = jnp.concatenate(
        [
            (peer[0].astype(jnp.float32) - own[0].astype(jnp.float32)).astype(jnp.bfloat16),
            (peer[1].astype(jnp.float32) - own[1].astype(jnp.float32)).astype(jnp.bfloat16),
        ],
        axis=0,
    )
    mixed = (
        rows.astype(jnp.float32) + inner + contract(weighted_map_ref[...], flux, 1, 0)
    ).astype(jnp.bfloat16)
    mixed_ref[...] = mixed
    mixed = mixed.astype(jnp.float32)
    inverse = lax.rsqrt(jnp.mean(mixed * mixed, axis=1, keepdims=True) + EPS)
    inverse_ref[...] = inverse
    normed_ref[...] = (mixed * inverse).astype(jnp.bfloat16)
    queries_ref[...] = contract(normed_ref[...], query_matrix_ref[...], 1, 0).astype(jnp.bfloat16)

    def take_pack(step, carry):
        pack_copy(step, lax.rem(me + count - step, count)).wait_recv()
        pack_copy(step, me).wait_send()
        return carry

    lax.fori_loop(1, count, take_pack, 0)
    gathered_ref[...] = landed[...]


def front(
    cells, first, second, weight, upper_cells, lower_cells, live, pack, cotangent, query_matrix, output_matrix
):
    count = lax.axis_size("blk")
    cell_count = cells.shape[0]
    slots = live.shape[0]
    line = lax.broadcasted_iota(jnp.int32, (8, 1), 0)
    table = lambda one, two: jnp.where(line == 0, one[None, :], two[None, :])
    inner_table = table(first, second)
    cross_table = table(upper_cells, lower_cells)
    live_table = jnp.broadcast_to(live[None, :], (8, slots))
    low_type = lambda *shape: jax.ShapeDtypeStruct(shape, jnp.bfloat16)
    return pl.pallas_call(
        functools.partial(front_kernel, count),
        in_specs=[pl.BlockSpec(memory_space=pltpu.VMEM)] * 9,
        out_specs=[pl.BlockSpec(memory_space=pltpu.VMEM)] * 10,
        out_shape=(
            low_type(*cells.shape),
            low_type(*cells.shape),
            jax.ShapeDtypeStruct((cell_count, 1), jnp.float32),
            low_type(cell_count, cell_count),
            low_type(cell_count, cell_count),
            low_type(cell_count, 2 * slots),
            low_type(cell_count, 2 * slots),
            low_type(count, *pack.shape),
            low_type(*cells.shape),
            low_type(*cells.shape),
        ),
        scratch_shapes=[
            pltpu.VMEM((2, slots, cells.shape[1]), jnp.bfloat16),
            pltpu.VMEM((2, slots, cells.shape[1]), jnp.bfloat16),
            pltpu.VMEM((8, slots), jnp.float32),
            pltpu.VMEM((count, *pack.shape), jnp.bfloat16),
            pltpu.SemaphoreType.DMA((count,)),
            pltpu.SemaphoreType.DMA((count,)),
            pltpu.SemaphoreType.DMA((3,)),
            pltpu.SemaphoreType.DMA((3,)),
        ],
        compiler_params=pltpu.CompilerParams(
            collective_id=0, has_side_effects=True, vmem_limit_bytes=(20 if count <= 32 else 28) * MIB
        ),
        cost_estimate=pl.CostEstimate(
            flops=8 * first.shape[0] * cell_count * cell_count,
            bytes_accessed=8 * cell_count * cell_count,
            transcendentals=0,
        ),
    )(
        cells,
        inner_table,
        weight[None, :],
        cross_table,
        live_table,
        pack,
        cotangent,
        query_matrix,
        output_matrix,
    )


def attention_kernel(
    scale,
    query_ref,
    grad_ref,
    key_ref,
    value_ref,
    cell_code_ref,
    anchor_code_ref,
    dead_ref,
    attended_ref,
    grad_query_ref,
    grad_key_ref,
    grad_value_ref,
):
    anchors = key_ref.shape[0]
    half = key_ref.shape[1] // 2
    left = lax.broadcasted_iota(jnp.int32, key_ref.shape, 1) < half

    def both(ref):
        rows = ref[...]
        none = jnp.zeros_like(rows)
        return jnp.concatenate([jnp.where(left, rows, none), jnp.where(left, none, rows)], axis=0)

    keys, values = both(key_ref), both(value_ref)
    queries, grads = query_ref[...], grad_ref[...]
    scores = contract(queries, keys, 1, 1)
    grad_prob = contract(grads, values, 1, 1)
    bias = cell_code_ref[...] * anchor_code_ref[...] + dead_ref[...]
    lows, grad_lows = [], []
    for head in range(2):
        part = slice(head * anchors, (head + 1) * anchors)
        score = scores[:, part] * scale + bias
        exp_scores = jnp.exp(score - jnp.max(score, axis=1, keepdims=True))
        weights = exp_scores * (1.0 / jnp.sum(exp_scores, axis=1, keepdims=True))
        low = weights.astype(jnp.bfloat16)
        gradient = grad_prob[:, part]
        dots = jnp.sum(low.astype(jnp.float32) * gradient, axis=1, keepdims=True)
        lows.append(low)
        grad_lows.append((weights * (gradient - dots)).astype(jnp.bfloat16))
    low = jnp.concatenate(lows, axis=1)
    grad_low = jnp.concatenate(grad_lows, axis=1)
    attended_ref[...] = contract(low, values, 1, 0).astype(jnp.bfloat16)
    grad_query_ref[...] = (contract(grad_low, keys, 1, 0) * scale).astype(jnp.bfloat16)
    upper = lax.broadcasted_iota(jnp.int32, grad_key_ref.shape, 0) < half
    grad_key = contract(queries, grad_low, 0, 0) * scale
    grad_key_ref[...] = jnp.where(upper, grad_key[:, :anchors], grad_key[:, anchors:])
    grad_value = contract(grads, low, 0, 0)
    grad_value_ref[...] = jnp.where(upper, grad_value[:, :anchors], grad_value[:, anchors:])


def attention(queries, grads, keyvals, cell_code, anchor_code, dead):
    cells = queries.shape[0]
    anchors = keyvals.shape[0]
    pairs = HEADS // 2
    wide = MODEL_WIDTH // pairs
    rows = pl.BlockSpec((cells, wide), lambda i: (0, i))
    keys = pl.BlockSpec((anchors, wide), lambda i: (0, i))
    values = pl.BlockSpec((anchors, wide), lambda i: (0, i + pairs))
    turned = pl.BlockSpec((wide, anchors), lambda i: (i, 0))
    fixed = lambda shape: pl.BlockSpec(shape, lambda i: (0, 0))
    limit = min(56 * MIB, 8 * MIB + 64 * cells * anchors)
    return pl.pallas_call(
        functools.partial(attention_kernel, 1.0 / math.sqrt(MODEL_WIDTH // HEADS)),
        grid=(pairs,),
        in_specs=[rows, rows, keys, values, fixed((cells, 1)), fixed((1, anchors)), fixed((1, anchors))],
        out_specs=[rows, rows, turned, turned],
        out_shape=(
            jax.ShapeDtypeStruct((cells, MODEL_WIDTH), jnp.bfloat16),
            jax.ShapeDtypeStruct((cells, MODEL_WIDTH), jnp.bfloat16),
            jax.ShapeDtypeStruct((MODEL_WIDTH, anchors), jnp.float32),
            jax.ShapeDtypeStruct((MODEL_WIDTH, anchors), jnp.float32),
        ),
        compiler_params=pltpu.CompilerParams(vmem_limit_bytes=limit),
        cost_estimate=pl.CostEstimate(
            flops=24 * cells * anchors * MODEL_WIDTH,
            bytes_accessed=8 * cells * MODEL_WIDTH,
            transcendentals=cells * anchors * HEADS,
        ),
    )(queries, grads, keyvals, keyvals, cell_code[:, None], anchor_code[None, :], dead[None, :])


def tail_kernel(
    count,
    cotangent_ref,
    attended_ref,
    grad_query_ref,
    normed_ref,
    mixed_ref,
    inverse_ref,
    query_matrix_ref,
    inner_high_ref,
    inner_low_ref,
    cross_map_ref,
    weighted_map_ref,
    grad_key_ref,
    grad_value_ref,
    output_matrix_ref,
    tokens_ref,
    layer_output_ref,
    cell_grads_ref,
    weight_grads_ref,
    query_sum,
    output_sum,
    key_sum,
    value_sum,
    own,
    peer,
    face_send,
    face_recv,
    sum_send,
    sum_recv,
    *buffers,
):
    me = lax.axis_index("blk")
    quarter = count // 4
    rows = 4 * MODEL_WIDTH // count
    slots = own.shape[1]
    stages = quarter.bit_length() - 1
    place = lax.div(me, quarter)
    barrier = pltpu.get_barrier_semaphore()

    def greet(step, carry):
        pl.semaphore_signal(
            barrier, inc=1, device_id={"blk": lax.rem(me + step, count)}, device_id_type=MESH
        )
        return carry

    lax.fori_loop(1, count, greet, 0)

    def upper_bit(bit):
        return lax.rem(lax.div(me, bit), 2)

    def copy(source, target, place_in_sems, bit):
        return pltpu.make_async_remote_copy(
            src_ref=source,
            dst_ref=target,
            send_sem=sum_send.at[place_in_sems],
            recv_sem=sum_recv.at[place_in_sems],
            device_id={"blk": me + bit - 2 * bit * upper_bit(bit)},
            device_id_type=MESH,
        )

    def send(stage, kind, total):
        half = quarter >> (stage + 1)
        bit = 1 << stage
        upper = upper_bit(bit)
        out, into = buffers[8 * stage + 2 * kind], buffers[8 * stage + 2 * kind + 1]
        for i in range(half):
            out[i] = total[2 * i + 1 - upper].astype(jnp.bfloat16)
            total[i] = total[2 * i + upper]
        moved = copy(out, into, 4 * stage + kind, bit)
        moved.start()

        def take():
            moved.wait()
            for i in range(half):
                total[i] = total[i] + into[i].astype(jnp.float32)

        return take

    totals = (output_sum, query_sum, key_sum, value_sum)
    shape = (quarter, rows, MODEL_WIDTH)
    output_sum[...] = contract(cotangent_ref[...], attended_ref[...], 0, 0).reshape(shape)
    key_sum[...] = grad_key_ref[...].reshape(key_sum.shape)
    value_sum[...] = grad_value_ref[...].reshape(value_sum.shape)
    pl.semaphore_wait(barrier, count - 1)
    waits = [send(0, 0, output_sum)]
    query_sum[...] = contract(grad_query_ref[...], normed_ref[...], 0, 0).reshape(shape)
    waits += [send(0, kind, totals[kind]) for kind in range(1, 4)]

    grad_normed = contract(grad_query_ref[...], query_matrix_ref[...], 1, 1)
    for stage in range(1, stages):
        following = []
        for kind in range(4):
            waits[kind]()
            following.append(send(stage, kind, totals[kind]))
        waits = following

    inverse = inverse_ref[...]
    normal_hat = mixed_ref[...].astype(jnp.float32) * inverse
    grad_mixed = (
        cotangent_ref[...].astype(jnp.float32)
        + inverse
        * (grad_normed - normal_hat * jnp.mean(grad_normed * normal_hat, axis=1, keepdims=True))
    ).astype(jnp.bfloat16)
    cell_grads_ref[...] = grad_mixed
    chosen = contract(cross_map_ref[...], grad_mixed, 0, 0)
    own[0] = chosen[:slots].astype(jnp.bfloat16)
    own[1] = chosen[slots:].astype(jnp.bfloat16)

    def sent(source, target, number, by):
        return pltpu.make_async_remote_copy(
            src_ref=source,
            dst_ref=target,
            send_sem=face_send.at[number],
            recv_sem=face_recv.at[number],
            device_id={"blk": lax.rem(me + by + count, count)},
            device_id_type=MESH,
        )

    down = sent(own.at[1], peer.at[0], 0, -1)
    up = sent(own.at[0], peer.at[1], 1, 1)

    @pl.when(me > 0)
    def _():
        down.start()

    @pl.when(me < count - 1)
    def _():
        up.start()

    @pl.when(me == 0)
    def _():
        peer[1] = jnp.zeros(peer.shape[1:], peer.dtype)

    @pl.when(me == count - 1)
    def _():
        peer[0] = jnp.zeros(peer.shape[1:], peer.dtype)

    result = (
        cell_grads_ref[...].astype(jnp.float32)
        + contract(inner_high_ref[...], cell_grads_ref[...], 1, 0)
        + contract(inner_low_ref[...], cell_grads_ref[...], 1, 0)
    )
    layer_output_ref[...] = (
        mixed_ref[...].astype(jnp.float32)
        + contract(attended_ref[...], output_matrix_ref[...], 1, 0)
    ).astype(jnp.bfloat16)
    for take in waits:
        take()
    wide_out, wide_in, pair_out, pair_in, last_out, last_in, last_pair_out, last_pair_in = buffers[
        8 * stages :
    ]
    odd = lax.rem(place, 2) > 0
    wide_out[...] = jnp.where(odd, query_sum[0], output_sum[0]).astype(jnp.bfloat16)
    pair_out[...] = jnp.where(odd, value_sum[0], key_sum[0]).astype(jnp.bfloat16)
    wide = copy(wide_out, wide_in, 4 * stages, quarter)
    pair = copy(pair_out, pair_in, 4 * stages + 1, quarter)
    wide.start()
    pair.start()
    wide_kept = jnp.where(odd, output_sum[0], query_sum[0])
    pair_kept = jnp.where(odd, key_sum[0], value_sum[0])

    @pl.when(me < count - 1)
    def _():
        down.wait_recv()
        up.wait_send()

    @pl.when(me > 0)
    def _():
        up.wait_recv()
        down.wait_send()

    flux = jnp.concatenate(
        [
            (peer[0].astype(jnp.float32) - own[0].astype(jnp.float32)).astype(jnp.bfloat16),
            (peer[1].astype(jnp.float32) - own[1].astype(jnp.float32)).astype(jnp.bfloat16),
        ],
        axis=0,
    )
    wide.wait()
    pair.wait()
    query_sum[0] = wide_kept + wide_in[...].astype(jnp.float32)
    key_sum[0] = pair_kept + pair_in[...].astype(jnp.float32)
    last = copy(last_out, last_in, 4 * stages + 2, 2 * quarter)
    last_pair = copy(last_pair_out, last_pair_in, 4 * stages + 3, 2 * quarter)
    outer = lax.rem(place + 1, 4) < 2
    inside = lax.rem(place + 1, 4) >= 2

    @pl.when(inside)
    def _():
        last_out[...] = query_sum[0].astype(jnp.bfloat16)
        last.start()

    @pl.when(outer)
    def _():
        last_pair_out[...] = key_sum[0].astype(jnp.bfloat16)
        last_pair.start()

    cell_grads_ref[...] = (result + contract(weighted_map_ref[...], flux, 1, 0)).astype(jnp.bfloat16)

    @pl.when(inside)
    def _():
        last_pair.wait_recv()
        total = key_sum[0] + last_pair_in[...].astype(jnp.float32)
        weight_grads_ref[...] = contract(
            total, tokens_ref[...].astype(jnp.float32), 1, 0, lax.Precision.HIGHEST
        )
        last.wait_send()

    @pl.when(outer)
    def _():
        last.wait_recv()
        weight_grads_ref[...] = query_sum[0] + last_in[...].astype(jnp.float32)
        last_pair.wait_send()


def tail(*operands):
    count = lax.axis_size("blk")
    cells = operands[0].shape
    anchors = operands[-1].shape[0]
    slots = operands[9].shape[1] // 2
    quarter = count // 4
    rows = 4 * MODEL_WIDTH // count
    stages = quarter.bit_length() - 1
    low = lambda *shape: pltpu.VMEM(shape, jnp.bfloat16)
    full = lambda *shape: pltpu.VMEM(shape, jnp.float32)
    buffers = []
    for stage in range(stages):
        half = quarter >> (stage + 1)
        buffers += [low(half, rows, MODEL_WIDTH)] * 4 + [low(half, rows, anchors)] * 4
    buffers += ([low(rows, MODEL_WIDTH)] * 2 + [low(rows, anchors)] * 2) * 2
    vmem = pl.BlockSpec(memory_space=pltpu.VMEM)
    return pl.pallas_call(
        functools.partial(tail_kernel, count),
        in_specs=[vmem] * len(operands),
        out_specs=[vmem] * 3,
        out_shape=(
            jax.ShapeDtypeStruct(cells, jnp.bfloat16),
            jax.ShapeDtypeStruct(cells, jnp.bfloat16),
            jax.ShapeDtypeStruct((rows, MODEL_WIDTH), jnp.float32),
        ),
        scratch_shapes=[
            full(quarter, rows, MODEL_WIDTH),
            full(quarter, rows, MODEL_WIDTH),
            full(quarter, rows, anchors),
            full(quarter, rows, anchors),
            low(2, slots, MODEL_WIDTH),
            low(2, slots, MODEL_WIDTH),
            pltpu.SemaphoreType.DMA((2,)),
            pltpu.SemaphoreType.DMA((2,)),
            pltpu.SemaphoreType.DMA((4 * stages + 4,)),
            pltpu.SemaphoreType.DMA((4 * stages + 4,)),
        ]
        + buffers,
        compiler_params=pltpu.CompilerParams(
            collective_id=1, has_side_effects=True, vmem_limit_bytes=(24 if count <= 32 else 44) * MIB
        ),
    )(*operands)


def shards(
    cell_features,
    cell_geometry_rows,
    anchor_token_features,
    anchor_geometry_rows,
    live_anchor_count,
    inner_face_first,
    inner_face_second,
    inner_face_weight,
    upper_face_cell,
    lower_face_cell,
    upper_face_weight,
    upper_slot_count,
    query_matrix,
    anchor_keyvalue_matrix,
    output_matrix,
    cotangent,
):
    own_anchors = anchor_token_features.shape[0]
    slot_index = jnp.arange(upper_face_cell.shape[0], dtype=jnp.int32)
    live_weight = jnp.where(
        slot_index < upper_slot_count[0], upper_face_weight.astype(jnp.float32), 0.0
    )
    live = jnp.arange(own_anchors, dtype=jnp.int32) < live_anchor_count[0]
    side = jnp.concatenate([anchor_geometry_rows, live.astype(jnp.bfloat16)])
    half_width = MODEL_WIDTH // 2
    pack = jnp.concatenate(
        [
            anchor_token_features.reshape(2 * own_anchors, half_width),
            jnp.broadcast_to(side[:, None], (2 * own_anchors, 128)),
        ],
        axis=1,
    )
    (
        mixed_rows,
        normed,
        inverse_rms,
        inner_high,
        inner_low,
        cross_map,
        weighted_map,
        packed,
        queries,
        attended_gradient,
    ) = front(
        cell_features,
        inner_face_first,
        inner_face_second,
        inner_face_weight,
        upper_face_cell,
        lower_face_cell,
        live_weight,
        pack,
        cotangent,
        query_matrix,
        output_matrix,
    )
    tokens = packed[:, :, :half_width].reshape(-1, MODEL_WIDTH)
    anchor_code = packed[:, :own_anchors, half_width].reshape(-1).astype(jnp.float32)
    dead = jnp.where(packed[:, own_anchors:, half_width] > 0, 0.0, -jnp.inf)
    dead = dead.reshape(-1).astype(jnp.float32)
    keyvals = contract(tokens, anchor_keyvalue_matrix, 1, 0).astype(jnp.bfloat16)
    attended, grad_queries, grad_keys, grad_values = attention(
        queries, attended_gradient, keyvals, cell_geometry_rows, anchor_code, dead
    )
    layer_output, cell_grads, weight_grads = tail(
        cotangent,
        attended,
        grad_queries,
        normed,
        mixed_rows,
        inverse_rms,
        query_matrix,
        inner_high,
        inner_low,
        cross_map,
        weighted_map,
        grad_keys,
        grad_values,
        output_matrix,
        tokens,
    )
    return (layer_output, cell_grads, weight_grads)


def solution(mesh):
    cells = P(("groups", "blk"))
    in_specs = (cells,) * 12 + (P(), P(), P(), cells)
    return jax.shard_map(
        shards, mesh=mesh, in_specs=in_specs, out_specs=(cells, cells, cells), check_vma=False
    )
```
